128 devices in a mesh: tr: 16 (over z, x), tc: 8 (over y, core).
Axes of the slice: x: 4, y: 4, z: 4, core: 2. Of those that a mesh axis runs over, the one named last changes fastest.
Arguments:
- tokens: bfloat16 [512, 256, 1280], P('tr', 'tc'), may hold values from -48 to 48
- norm_gain: float32 [1280], replicated, may hold values from 0.5 to 1.5
- window_weight: bfloat16 [1280, 3840], replicated, may hold values from -20 to 20
- output_weight: bfloat16 [1280, 1280], replicated, may hold values from -0.15625 to 0.15625
- token_slot: int32 [512, 256], P('tr', 'tc'), may hold values from 0 to 23, as said below
- block_parcel: int32 [128, 8, 24], P('tr', 'tc'), may hold values from -1 to 16383, as said below
- parcel_place: int32 [16384], replicated, may hold values from 0 to 16383, as said below
- parcel_class: int32 [16384], replicated, may hold values from 0 to 7
- pool_exponent: float32 [8], replicated, may hold values from 1.5 to 5
- embed_weight: bfloat16 [1280, 1024], replicated, may hold values from -0.15625 to 0.15625
- parcel_gain: float32 [1024], replicated, may hold values from 0.5 to 1.5
- parcel_weight: bfloat16 [3, 1024, 1024], P(None, None, 'tc'), may hold values from -8 to 8
- merge_weight: bfloat16 [1024, 1024], P('tc'), may hold values from -0.1875 to 0.1875
- adjacency: int32 [128, 4], replicated, may hold values from 0 to 127, as said below
Outputs:
- tile_output: bfloat16 [512, 256, 1280], P('tr', 'tc')
- parcel_vector: bfloat16 [16384, 1024], P(('tr', 'tc'))
The draws below stay inside these ranges and needn't reach their ends.
Inputs may be any that keep to these rules, and one draw needn't show every extreme that they name: `token_slot`: in every token block, the slots take each value from 0 to m - 1 at least once and never fall in row-major order, where m is the number of non-negative entries of that block's row of block_parcel. `block_parcel`: A row lists m distinct parcel ids followed by 24 - m entries -1, with m from 8 to 24; every device has a block with m = 24. Every parcel appears in exactly one block, and the blocks of one device list 128 parcels in all. `parcel_place`: A permutation. Table rows k * 128 to (k + 1) * 128 - 1 belong to device k, devices counted along tr then tc. Of the parcels listed by one device's blocks, at most 2 belong to any one device, and exactly 2 for some device of each device's. `adjacency`: row b starts with b itself; the other 3 entries are distinct blocks of other owner rows (block c belongs to owner row c // 8). Together the lists of one owner row's blocks name at most 2 distinct blocks of any other owner row, and exactly 2 of some other owner row.
All inputs are finite; a program needn't handle non-finite values.
Results may differ from the reference program's by a relative error of at most 0.019.
Values may be sent and summed in bfloat16 or wider, within the bound.
A program may use at most 192 MiB of HBM per device.

```python
import math
import jax
import jax.numpy as jnp
from jax import lax

D = 1280
HEADS = 16
HDIM = 80
WIN = 8
SHIFT = 4
TH = 32
TW = 32
BLOCK = 128
BROWS = 4
PPB = 16
KSLOT = 24
NCLASS = 8
PARCELS_DEV = 128
NR = 512
NC = 256
PARCELS = 16384
D2 = 1024
P_HEADS = 8
P_HDIM = 128
PB = 128
BLK_OWN = 8
NBLK = 128
NB = 4
MAXB = 2
N_TR = 16
N_TC = 8


def parcel_layout(key):
    devices = N_TR * N_TC
    device_blocks = TH // BROWS
    halves = device_blocks // 2
    keys_all = jax.random.split(jax.random.fold_in(key, 101), 8)
    spread = jax.random.randint(keys_all[0], (devices, halves), 0, PPB // 2 + 1)
    full_at = jax.random.randint(keys_all[1], (devices, 1), 0, halves)
    spread = jnp.where(jnp.arange(halves)[None, :] == full_at, PPB // 2, spread)
    block_sizes = jnp.stack([PPB + spread, PPB - spread], axis=2).reshape(devices, device_blocks)
    starts = jnp.cumsum(block_sizes, axis=1) - block_sizes
    slot_index = jnp.arange(KSLOT)
    parcel_ids = jnp.arange(devices)[:, None, None] * PARCELS_DEV + starts[:, :, None] + slot_index
    block_ids = jnp.where(slot_index < block_sizes[:, :, None], parcel_ids, -1)
    token_index = jnp.arange(BLOCK)
    extra_slot = jax.random.randint(keys_all[2], (devices, device_blocks, BLOCK), 0, block_sizes[:, :, None])
    raw_slots = jnp.where(token_index < block_sizes[:, :, None], token_index, extra_slot)
    slot_values = jnp.sort(raw_slots, axis=2)
    block_array = block_ids.reshape(N_TR, N_TC, device_blocks, KSLOT).transpose(0, 2, 1, 3).reshape(N_TR * device_blocks, N_TC, KSLOT)
    slot_array = slot_values.reshape(N_TR, N_TC, device_blocks, BROWS, TW).transpose(0, 2, 3, 1, 4).reshape(NR, NC)
    base_count = PARCELS_DEV // devices
    lift_sizes = jax.random.randint(keys_all[3], (devices // 2,), 0, base_count + 1)
    lift_sizes = lift_sizes.at[0].set(base_count)
    pattern = jnp.stack([base_count + lift_sizes, base_count - lift_sizes], axis=1).reshape(devices)
    pattern = jax.random.permutation(keys_all[4], pattern)
    shifts = jax.random.permutation(keys_all[5], devices)
    counts = pattern[(jnp.arange(devices)[None, :] + shifts[:, None]) % devices]
    bounds = jnp.cumsum(counts, axis=1)
    sorted_owner = jnp.sum(jnp.arange(PARCELS_DEV)[None, :, None] >= bounds[:, None, :], axis=2)
    order_perm = jax.vmap(lambda sub_key: jax.random.permutation(sub_key, PARCELS_DEV))(jax.random.split(keys_all[6], devices))
    owner_label = jnp.take_along_axis(sorted_owner, order_perm, axis=1)
    first_pos = bounds - counts
    within = order_perm - jnp.take_along_axis(first_pos, owner_label, axis=1)
    before = jnp.cumsum(counts, axis=0) - counts
    local_pos = jnp.take_along_axis(before, owner_label, axis=1) + within
    shuffle = jax.vmap(lambda sub_key: jax.random.permutation(sub_key, PARCELS_DEV))(jax.random.split(keys_all[7], devices))
    local_pos = shuffle[owner_label, local_pos]
    place_rows = (owner_label * PARCELS_DEV + local_pos).reshape(devices * PARCELS_DEV)
    return (slot_array.astype(jnp.int32), block_array.astype(jnp.int32), place_rows.astype(jnp.int32))


def draw_token_slot(key, part):
    slot_array, block_array, place_rows = parcel_layout(key)
    return slot_array


def draw_block_parcel(key, part):
    slot_array, block_array, place_rows = parcel_layout(key)
    return block_array


def draw_parcel_place(key, part):
    slot_array, block_array, place_rows = parcel_layout(key)
    return place_rows


def draw_adjacency(key, part):
    key = jax.random.fold_in(key, 7)
    keys_all = jax.random.split(key, 4)
    others = N_TR - 1
    candidate_total = others * MAXB
    cand_local = jax.vmap(lambda sub_key: jax.random.permutation(sub_key, BLK_OWN))(jax.random.split(keys_all[0], N_TR * others))
    cand_local = cand_local[:, :MAXB].reshape(N_TR, others, MAXB)
    owner_of = (jnp.arange(N_TR)[:, None] + 1 + jnp.arange(others)[None, :]) % N_TR
    candidates = (owner_of[:, :, None] * BLK_OWN + cand_local).reshape(N_TR, candidate_total)
    scores = jax.vmap(lambda sub_key: jax.random.permutation(sub_key, candidate_total))(jax.random.split(keys_all[1], N_TR * BLK_OWN))
    scores = scores.reshape(N_TR, BLK_OWN, candidate_total)
    forced_block = jax.random.randint(keys_all[2], (N_TR,), 0, BLK_OWN)
    forced_owner = jax.random.randint(keys_all[3], (N_TR,), 0, others)
    cand_owner = jnp.repeat(jnp.arange(others), MAXB)
    is_forced = (jnp.arange(BLK_OWN)[None, :, None] == forced_block[:, None, None]) & (cand_owner[None, None, :] == forced_owner[:, None, None])
    scores = jnp.where(is_forced, -1 - (jnp.arange(candidate_total) % MAXB)[None, None, :], scores)
    chosen = jnp.argsort(scores, axis=2, stable=True)[:, :, :NB - 1]
    picked = jnp.take_along_axis(jnp.broadcast_to(candidates[:, None, :], (N_TR, BLK_OWN, candidate_total)), chosen, axis=2)
    self_block = jnp.arange(NBLK).reshape(N_TR, BLK_OWN, 1)
    return jnp.concatenate([self_block, picked], axis=2).reshape(NBLK, NB).astype(jnp.int32)


def draw_tokens(key, part):
    key = jax.random.fold_in(key, 11)
    keys_all = jax.random.split(key, 1)
    values = jnp.clip(jax.random.normal(keys_all[0], (NR, NC, D)), -8.0, 8.0)
    return values.astype(jnp.bfloat16)


def draw_window_weight(key, part):
    key = jax.random.fold_in(key, 13)
    keys_all = jax.random.split(key, 1)
    raw_weight = jnp.clip(jax.random.normal(keys_all[0], (D, 3 * D)), -6.0, 6.0) * D ** (-0.5)
    return raw_weight.astype(jnp.bfloat16)


def draw_parcel_weight(key, part):
    key = jax.random.fold_in(key, 17)
    keys_all = jax.random.split(key, 1)
    raw_weight = jnp.clip(jax.random.normal(keys_all[0], (3, D2, D2)), -6.0, 6.0) * D2 ** (-0.5)
    return raw_weight.astype(jnp.bfloat16)


def plant(array, stream_key, smallest, high):
    longest = array.shape.index(max(array.shape))
    spots = []
    for shift in (0, 1):
        where = [jax.random.randint(jax.random.fold_in(stream_key, axis), (), 0, length) for axis, length in enumerate(array.shape)]
        where[longest] = (where[longest] + shift) % array.shape[longest]
        spots.append(tuple(where))
    return array.at[spots[0]].set(smallest).at[spots[1]].set(high)


def levels(stream_key, extent, shards, least, high):
    def one(dim, blocks):
        steps = jax.random.uniform(jax.random.fold_in(jax.random.fold_in(stream_key, 6), dim), (blocks,), jnp.float32, least / len(shards), high / len(shards))
        return jnp.repeat(jnp.exp(steps), extent[dim] // blocks).reshape((-1,) + (1,) * (len(extent) - dim - 1))

    factor_of = one(*shards[0])
    for cut in shards[1:]:
        factor_of = factor_of * one(*cut)
    return factor_of


def normal_values(own_key, dims, scale, bound, cuts=(), kind=jnp.bfloat16):
    array = jax.random.normal(own_key, dims, jnp.float32) * scale
    if len(cuts) > 0:
        array = levels(own_key, dims, cuts, -0.22, 0.18) * array
    return jnp.clip(array, min=-bound, max=bound).astype(kind)


def setup_inputs(seed: int = 0) -> dict:
    key_list = jax.random.split(jax.random.key(seed), 15)
    tokens = draw_tokens(jax.random.fold_in(key_list[14], 71), 0)
    norm_gain = jnp.clip(1.0 + 0.1 * jax.random.normal(key_list[1], (D,), jnp.float32), 0.5, 1.5)
    window_weight = draw_window_weight(jax.random.fold_in(key_list[14], 71), 0)
    output_weight = normal_values(key_list[3], (D, D), D ** -0.5, 0.15625)
    token_slot = draw_token_slot(jax.random.fold_in(key_list[14], 71), 0)
    block_parcel = draw_block_parcel(jax.random.fold_in(key_list[14], 71), 0)
    parcel_place = draw_parcel_place(jax.random.fold_in(key_list[14], 71), 0)
    parcel_class = plant(jax.random.randint(key_list[7], (PARCELS,), 0, NCLASS), jax.random.fold_in(key_list[7], 1), 0, NCLASS - 1).astype(jnp.int32)
    pool_exponent = jnp.clip(jnp.exp(jax.random.uniform(key_list[8], (NCLASS,), jnp.float32, math.log(1.5), math.log(5.0))), 1.5, 5.0)
    embed_weight = normal_values(key_list[9], (D, D2), D ** -0.5, 0.15625)
    parcel_gain = jnp.clip(1.0 + 0.1 * jax.random.normal(key_list[10], (D2,), jnp.float32), 0.5, 1.5)
    parcel_weight = draw_parcel_weight(jax.random.fold_in(key_list[14], 71), 0)
    merge_weight = normal_values(key_list[12], (D2, D2), D2 ** -0.5, 0.1875, ((0, 8),))
    adjacency = draw_adjacency(jax.random.fold_in(key_list[14], 71), 0)
    return dict(tokens=tokens, norm_gain=norm_gain, window_weight=window_weight, output_weight=output_weight, token_slot=token_slot, block_parcel=block_parcel, parcel_place=parcel_place, parcel_class=parcel_class, pool_exponent=pool_exponent, embed_weight=embed_weight, parcel_gain=parcel_gain, parcel_weight=parcel_weight, merge_weight=merge_weight, adjacency=adjacency)


norm_epsilon = 1e-05
pool_floor = 1e-06

def layer_norm(values, norm_gain):
    centred = values - lax.optimization_barrier(jnp.mean(values, axis=-1, keepdims=True))
    spread = lax.optimization_barrier(jnp.mean(centred * centred, axis=-1, keepdims=True))
    return centred * lax.rsqrt(spread + norm_epsilon) * norm_gain

def softmax_rows(scores):
    row_top = lax.optimization_barrier(jnp.max(scores, axis=-1, keepdims=True))
    lifted = jnp.exp(scores - row_top)
    return lifted / lax.optimization_barrier(jnp.sum(lifted, axis=-1, keepdims=True))

def window_strip(strip_rows, strip_index, norm_gain, window_weight, output_weight):
    width_cols = NC + 2 * SHIFT
    windows = width_cols // WIN
    normed = layer_norm(strip_rows.astype(jnp.float32), norm_gain).astype(jnp.bfloat16)
    packed = jnp.dot(normed.reshape(WIN * width_cols, D), window_weight, preferred_element_type=jnp.float32).astype(jnp.bfloat16)
    packed = packed.reshape(WIN, windows, WIN, 3, HEADS, HDIM).transpose(1, 0, 2, 3, 4, 5)
    packed = packed.reshape(windows, WIN * WIN, 3, HEADS, HDIM)
    queries = packed[:, :, 0].astype(jnp.float32)
    key_rows = packed[:, :, 1].astype(jnp.float32)
    value_rows = packed[:, :, 2].astype(jnp.float32)
    row_global = strip_index * WIN + jnp.arange(WIN, dtype=jnp.int32) - SHIFT
    col_global = jnp.arange(width_cols, dtype=jnp.int32) - SHIFT
    row_valid = (row_global >= 0) & (row_global < NR)
    col_valid = (col_global >= 0) & (col_global < NC)
    key_valid = (row_valid[:, None] & col_valid[None, :]).reshape(WIN, windows, WIN).transpose(1, 0, 2)
    key_valid = key_valid.reshape(windows, WIN * WIN)
    scores = jnp.einsum('wqhd,wkhd->whqk', queries, key_rows) * HDIM ** (-0.5)
    scores = jnp.where(key_valid[:, None, None, :], scores, -jnp.inf)
    weights = softmax_rows(scores).astype(jnp.bfloat16)
    mixed_rows = jnp.einsum('whqk,wkhd->wqhd', weights.astype(jnp.float32), value_rows).astype(jnp.bfloat16)
    mixed_rows = mixed_rows.reshape(windows, WIN, WIN, D).transpose(1, 0, 2, 3).reshape(WIN * width_cols, D)
    result = jnp.dot(mixed_rows, output_weight, preferred_element_type=jnp.float32)
    result = result + strip_rows.reshape(WIN * width_cols, D).astype(jnp.float32)
    return result.astype(jnp.bfloat16).reshape(WIN, width_cols, D)

def reference(tokens, norm_gain, window_weight, output_weight, token_slot, block_parcel, parcel_place, parcel_class, pool_exponent, embed_weight, parcel_gain, parcel_weight, merge_weight, adjacency):
    padded = jnp.pad(tokens, ((SHIFT, SHIFT), (SHIFT, SHIFT), (0, 0)))
    strip_total = NR // WIN + 1
    strips = padded.reshape(strip_total, WIN, NC + 2 * SHIFT, D)
    finished = lax.map(lambda strip_pair: window_strip(strip_pair[0], strip_pair[1], norm_gain, window_weight, output_weight), (strips, jnp.arange(strip_total, dtype=jnp.int32)))
    finished = finished.reshape(NR + 2 * SHIFT, NC + 2 * SHIFT, D)
    tile_output = finished[SHIFT:SHIFT + NR, SHIFT:SHIFT + NC]
    block_rows = NR // BROWS
    feature_blocks = tile_output.reshape(block_rows, BROWS, N_TC, TW, D).transpose(0, 2, 1, 3, 4).reshape(block_rows, N_TC, BLOCK, D)
    slot_blocks = token_slot.reshape(block_rows, BROWS, N_TC, TW).transpose(0, 2, 1, 3).reshape(block_rows, N_TC, BLOCK)

    def accumulate(carried, block_inputs):
        power_sums, token_counts = carried
        features, slot_values, parcel_ids = block_inputs
        live_slot = parcel_ids >= 0
        places = parcel_place[jnp.maximum(parcel_ids, 0)]
        exponent = pool_exponent[parcel_class[places]]
        onehot = (slot_values[..., None] == jnp.arange(KSLOT, dtype=jnp.int32)).astype(jnp.float32)
        token_power = lax.optimization_barrier(jnp.sum(onehot * exponent[:, None, :], axis=-1))
        lifted = jnp.exp(token_power[..., None] * jnp.log(jnp.maximum(features.astype(jnp.float32), pool_floor)))
        block_sums = jnp.einsum('cts,ctd->csd', onehot, lifted, precision=lax.Precision.HIGHEST)
        block_counts = lax.optimization_barrier(jnp.sum(onehot, axis=1))
        target = jnp.where(live_slot, places, PARCELS).reshape(-1)
        power_sums = power_sums.at[target].add(block_sums.reshape(-1, D), mode='drop')
        token_counts = token_counts.at[target].add(block_counts.reshape(-1), mode='drop')
        return ((power_sums, token_counts), None)
    initial = (jnp.zeros((PARCELS, D), jnp.float32), jnp.zeros((PARCELS,), jnp.float32))
    (power_sums, token_counts), unused = lax.scan(accumulate, initial, (feature_blocks, slot_blocks, block_parcel))
    parcel_power = pool_exponent[parcel_class]
    pooled = jnp.exp(jnp.log(power_sums / token_counts[:, None]) / parcel_power[:, None]).astype(jnp.bfloat16)
    hidden_rows = jnp.dot(pooled, embed_weight, preferred_element_type=jnp.float32).astype(jnp.bfloat16)
    normed_rows = layer_norm(hidden_rows.astype(jnp.float32), parcel_gain).astype(jnp.bfloat16)
    queries = jnp.dot(normed_rows, parcel_weight[0], preferred_element_type=jnp.float32).astype(jnp.bfloat16)
    key_rows = jnp.dot(normed_rows, parcel_weight[1], preferred_element_type=jnp.float32).astype(jnp.bfloat16)
    value_rows = jnp.dot(normed_rows, parcel_weight[2], preferred_element_type=jnp.float32).astype(jnp.bfloat16)
    key_blocks = key_rows.reshape(NBLK, PB, D2)
    value_blocks = value_rows.reshape(NBLK, PB, D2)
    query_blocks = queries.reshape(NBLK, PB, P_HEADS, P_HDIM)

    def attend(block_inputs):
        query_block, neighbours = block_inputs
        near_keys = key_blocks[neighbours].reshape(NB * PB, P_HEADS, P_HDIM).astype(jnp.float32)
        near_values = value_blocks[neighbours].reshape(NB * PB, P_HEADS, P_HDIM).astype(jnp.float32)
        scores = jnp.einsum('qhd,khd->hqk', query_block.astype(jnp.float32), near_keys) * P_HDIM ** (-0.5)
        weights = softmax_rows(scores).astype(jnp.bfloat16)
        return jnp.einsum('hqk,khd->qhd', weights.astype(jnp.float32), near_values).astype(jnp.bfloat16)
    attended = lax.map(attend, (query_blocks, adjacency)).reshape(PARCELS, D2)
    group_width = D2 // N_TC
    summed = jnp.zeros((PARCELS, D2), jnp.float32)
    for group_index in range(N_TC):
        low = group_index * group_width
        group_term = jnp.dot(attended[:, low:low + group_width], merge_weight[low:low + group_width], preferred_element_type=jnp.float32).astype(jnp.bfloat16)
        summed = summed + group_term.astype(jnp.float32)
    parcel_vector = (summed + hidden_rows.astype(jnp.float32)).astype(jnp.bfloat16)
    return (tile_output, parcel_vector)
```

```python
import jax
import jax.numpy as jnp
from jax import lax
from jax.experimental import pallas as pl
from jax.experimental.pallas import tpu as pltpu
from jax.sharding import PartitionSpec as P

HEADS = 16
HDIM = 80
WIN = 8
SHIFT = 4
BLOCK = 128
KSLOT = 24
NCLASS = 8
PARCELS_DEV = 128
P_HDIM = 128
PB = 128
NB = 4
MAXB = 2


norm_epsilon = 1e-05
pool_floor = 1e-06


def layer_norm(values, norm_gain):
    centred = values - jnp.mean(values, axis=-1, keepdims=True)
    spread = jnp.mean(centred * centred, axis=-1, keepdims=True)
    return centred * lax.rsqrt(spread + norm_epsilon) * norm_gain


def softmax_rows(scores):
    row_top = jnp.max(scores, axis=-1, keepdims=True)
    lifted = jnp.exp(scores - row_top)
    return lifted / jnp.sum(lifted, axis=-1, keepdims=True)


MESH = pl.DeviceIdType.MESH
GROUP = 640
SUB = 16
DIRECTIONS = ((-1, -1), (-1, 0), (-1, 1), (0, -1), (0, 1), (1, -1), (1, 0), (1, 1))
SCALE = HDIM ** (-0.5) * 1.4426950408889634


def strip_perm(flip):
    first = lax.broadcasted_iota(jnp.int32, (BLOCK, BLOCK), 0)
    second = lax.broadcasted_iota(jnp.int32, (BLOCK, BLOCK), 1)
    out_at, in_at = (second, first) if flip else (first, second)
    source = ((out_at // 4) % 4) * 32 + (out_at // 16) * 4 + out_at % 4
    return jnp.where(source == in_at, 1.0, 0.0).astype(jnp.bfloat16)


def halo_part(step, width):
    if step == 0:
        return pl.ds(1, width), pl.ds(1, width)
    if step == 1:
        return pl.ds(width, 1), pl.ds(0, 1)
    return pl.ds(1, 1), pl.ds(width + 1, 1)


def window_pairs(qkv, group, key_at, query_at, out_at, mixed, bias):
    lane = lax.broadcasted_iota(jnp.int32, (1, 256), 1)
    low = lax.broadcasted_iota(jnp.int32, (1, 128), 1) < 64
    parts = [None] * 5
    sums = [None] * 5
    rows = query_at[2] * query_at[3] * SUB
    for pair in range(4):
        lanes = pl.ds(128 * pair, 256)
        query = qkv[group, pl.ds(query_at[0], query_at[2]), pl.ds(query_at[1], query_at[3]), :, lanes]
        query = query.reshape(rows, 256)
        keys = qkv[2 + group, pl.ds(key_at[0], 2), pl.ds(key_at[1], 2), :, lanes].reshape(64, 256)
        vals = qkv[4 + group, pl.ds(key_at[0], 2), pl.ds(key_at[1], 2), :, lanes].reshape(64, 256)
        start = 32 * pair
        even = (lane >= start) & (lane < start + HDIM)
        odd = (lane >= start + HDIM) & (lane < start + 2 * HDIM)
        zero = jnp.zeros((), jnp.bfloat16)
        both_keys = jnp.concatenate([jnp.where(even, keys, zero), jnp.where(odd, keys, zero)], axis=0)
        both_vals = jnp.concatenate([jnp.where(even, vals, zero), jnp.where(odd, vals, zero)], axis=0)
        ones = jnp.ones((64, 256), jnp.bfloat16)
        both_ones = jnp.concatenate([jnp.where(even, ones, zero), jnp.where(odd, ones, zero)], axis=0)
        scores = lax.dot_general(
            query, both_keys, (((1,), (1,)), ((), ())), preferred_element_type=jnp.float32
        )
        if bias is not None:
            scores = scores + bias
        top_low = jnp.max(jnp.where(low, scores, -jnp.inf), axis=-1, keepdims=True)
        top_high = jnp.max(jnp.where(low, -jnp.inf, scores), axis=-1, keepdims=True)
        lifted = jnp.exp2((scores - jnp.where(low, top_low, top_high)) * SCALE).astype(jnp.bfloat16)
        part = jnp.dot(lifted, both_vals, preferred_element_type=jnp.float32)
        total = jnp.dot(lifted, both_ones, preferred_element_type=jnp.float32)
        for half in range(2):
            at = pair + half
            cut = slice(128 * half, 128 * half + 128)
            parts[at] = part[:, cut] if parts[at] is None else parts[at] + part[:, cut]
            sums[at] = total[:, cut] if sums[at] is None else sums[at] + total[:, cut]
    for at in range(5):
        tile = (parts[at] / sums[at]).astype(jnp.bfloat16)
        mixed[group, pl.ds(out_at[0], query_at[2]), pl.ds(out_at[1], query_at[3]), :, pl.ds(128 * at, 128)] = (
            tile.reshape(query_at[2], query_at[3], SUB, 128)
        )


def window_kernel(
    tokens_hbm, gain_ref, packed_weight_hbm, out_weight_hbm, out_hbm,
    tokens, ext, qkv, mixed, packed_weight, out_weight,
    token_sem, weight_sem, out_sem, send_sem, recv_sem,
):
    row = lax.axis_index("tr")
    col = lax.axis_index("tc")
    n_row = lax.axis_size("tr")
    n_col = lax.axis_size("tc")

    def token_copy(strip):
        return pltpu.make_async_copy(tokens_hbm.at[strip], tokens.at[strip], token_sem.at[strip])

    def weight_copy(chunk):
        return pltpu.make_async_copy(
            packed_weight_hbm.at[:, pl.ds(pl.multiple_of(GROUP * chunk, 128), GROUP)],
            packed_weight.at[chunk],
            weight_sem.at[chunk],
        )

    out_weight_copy = pltpu.make_async_copy(out_weight_hbm, out_weight, weight_sem.at[6])

    def result_copy(strip):
        return pltpu.make_async_copy(tokens.at[strip], out_hbm.at[strip], out_sem.at[strip])

    for strip in range(8):
        token_copy(strip).start()
    for chunk in range(6):
        weight_copy(chunk).start()
    out_weight_copy.start()

    barrier = pltpu.get_barrier_semaphore()
    peers = [
        {"tr": lax.rem(row + dr + n_row, n_row), "tc": lax.rem(col + dc + n_col, n_col)}
        for dr, dc in DIRECTIONS
    ]
    for peer in peers:
        pl.semaphore_signal(barrier, inc=1, device_id=peer, device_id_type=MESH)

    forward = strip_perm(False)

    @pl.loop(0, 8)
    def _(strip):
        token_copy(strip).wait()
        values = jnp.dot(forward, tokens[strip], preferred_element_type=jnp.float32)
        normed = layer_norm(values, gain_ref[...]).astype(jnp.bfloat16)
        ext[strip + 1, pl.ds(1, 8)] = normed.reshape(8, SUB, 1280)

    pl.semaphore_wait(barrier, 8)
    copies = []
    for k, (dr, dc) in enumerate(DIRECTIONS):
        (from_row, to_row), (from_col, to_col) = halo_part(dr, 8), halo_part(dc, 8)
        copies.append(
            pltpu.make_async_remote_copy(
                src_ref=ext.at[from_row, from_col],
                dst_ref=ext.at[to_row, to_col],
                send_sem=send_sem.at[k],
                recv_sem=recv_sem.at[k],
                device_id=peers[k],
                device_id_type=MESH,
            )
        )
    for copy in copies:
        copy.start()

    @pl.loop(0, 6)
    def _(chunk):
        weight_copy(chunk).wait()

        @pl.loop(0, 2)
        def _(part):
            source = ext[pl.ds(1 + 4 * part, 4), pl.ds(1, 8)].reshape(512, 1280)
            packed = jnp.dot(source, packed_weight[chunk], preferred_element_type=jnp.float32)
            qkv[chunk, pl.ds(1 + 4 * part, 4), pl.ds(1, 8)] = packed.astype(jnp.bfloat16).reshape(4, 8, SUB, GROUP)

    for copy in copies:
        copy.wait_recv()

    @pl.loop(2, 6)
    def _(chunk):
        source = jnp.concatenate(
            [
                ext[0].reshape(160, 1280),
                ext[9].reshape(160, 1280),
                ext[pl.ds(1, 8), 0].reshape(128, 1280),
                ext[pl.ds(1, 8), 9].reshape(128, 1280),
            ],
            axis=0,
        )
        packed = jnp.dot(source, packed_weight[chunk], preferred_element_type=jnp.float32).astype(jnp.bfloat16)
        qkv[chunk, 0] = packed[0:160].reshape(10, SUB, GROUP)
        qkv[chunk, 9] = packed[160:320].reshape(10, SUB, GROUP)
        qkv[chunk, pl.ds(1, 8), 0] = packed[320:448].reshape(8, SUB, GROUP)
        qkv[chunk, pl.ds(1, 8), 9] = packed[448:576].reshape(8, SUB, GROUP)

    key_lane = lax.broadcasted_iota(jnp.int32, (1, 128), 1)
    upper = (key_lane // 32) % 2 == 0
    left = (key_lane // 16) % 2 == 0

    def bias_of(bad):
        return jnp.where(bad, -1e30, 0.0)

    @pl.loop(0, 2)
    def _(group):
        @pl.loop(0, 9)
        def _(window):
            a, b = window // 3 + 1, window % 3 + 1
            window_pairs(
                qkv, group, (2 * a, 2 * b), (2 * a, 2 * b, 2, 2), (2 * a - 1, 2 * b - 1), mixed, None
            )

        @pl.loop(0, 6)
        def _(window):
            side, b = window // 3, window % 3 + 1
            edge = ((side == 0) & (row == 0)) | ((side == 1) & (row == n_row - 1))
            bias = bias_of((upper == (side == 0)) & edge)
            window_pairs(
                qkv, group, (8 * side, 2 * b), (1 + 7 * side, 2 * b, 1, 2), (7 * side, 2 * b - 1), mixed, bias
            )

        @pl.loop(0, 6)
        def _(window):
            side, a = window // 3, window % 3 + 1
            edge = ((side == 0) & (col == 0)) | ((side == 1) & (col == n_col - 1))
            bias = bias_of((left == (side == 0)) & edge)
            window_pairs(
                qkv, group, (2 * a, 8 * side), (2 * a, 1 + 7 * side, 2, 1), (2 * a - 1, 7 * side), mixed, bias
            )

        @pl.loop(0, 4)
        def _(window):
            down, across = window // 2, window % 2
            edge_row = ((down == 0) & (row == 0)) | ((down == 1) & (row == n_row - 1))
            edge_col = ((across == 0) & (col == 0)) | ((across == 1) & (col == n_col - 1))
            bias = bias_of(((upper == (down == 0)) & edge_row) | ((left == (across == 0)) & edge_col))
            window_pairs(
                qkv, group, (8 * down, 8 * across), (1 + 7 * down, 1 + 7 * across, 1, 1),
                (7 * down, 7 * across), mixed, bias,
            )

    out_weight_copy.wait()
    backward = strip_perm(True)

    @pl.loop(0, 4)
    def _(part):
        sources = []
        for half in range(2):
            strip = 2 * part + half
            packed = jnp.concatenate(
                [mixed[0, strip].reshape(BLOCK, GROUP), mixed[1, strip].reshape(BLOCK, GROUP)], axis=1
            )
            sources.append(jnp.dot(backward, packed, preferred_element_type=jnp.float32).astype(jnp.bfloat16))
        layer_out = jnp.dot(
            jnp.concatenate(sources, axis=0), out_weight[...], preferred_element_type=jnp.float32
        )
        for half in range(2):
            strip = 2 * part + half
            tokens[strip] = (
                layer_out[BLOCK * half : BLOCK * half + BLOCK] + tokens[strip].astype(jnp.float32)
            ).astype(jnp.bfloat16)
            result_copy(strip).start()

    for strip in range(8):
        result_copy(strip).wait()
    for copy in copies:
        copy.wait_send()


def encode_tile(tokens, norm_gain, window_weight, output_weight):
    tile_rows, tile_cols, width = tokens.shape
    anywhere = pl.BlockSpec(memory_space=pl.ANY)
    inside = pl.BlockSpec(memory_space=pltpu.VMEM)
    bf16 = jnp.bfloat16
    out = pl.pallas_call(
        window_kernel,
        out_shape=jax.ShapeDtypeStruct((8, BLOCK, width), bf16),
        in_specs=[anywhere, inside, anywhere, anywhere],
        out_specs=anywhere,
        scratch_shapes=[
            pltpu.VMEM((8, BLOCK, width), bf16),
            pltpu.VMEM((10, 10, SUB, width), bf16),
            pltpu.VMEM((6, 10, 10, SUB, GROUP), bf16),
            pltpu.VMEM((2, 8, 8, SUB, GROUP), bf16),
            pltpu.VMEM((6, width, GROUP), bf16),
            pltpu.VMEM((width, width), bf16),
            pltpu.SemaphoreType.DMA((8,)),
            pltpu.SemaphoreType.DMA((7,)),
            pltpu.SemaphoreType.DMA((8,)),
            pltpu.SemaphoreType.DMA((8,)),
            pltpu.SemaphoreType.DMA((8,)),
        ],
        compiler_params=pltpu.CompilerParams(
            collective_id=1, has_side_effects=True, vmem_limit_bytes=58 * 1024 * 1024
        ),
        cost_estimate=pl.CostEstimate(flops=20 * 10**9, bytes_accessed=20 * 10**6, transcendentals=2 * 10**6),
        name="window_attention",
    )(tokens.reshape(8, BLOCK, width), norm_gain.reshape(1, width), window_weight, output_weight)
    return out.reshape(tile_rows, tile_cols, width)


def body(
    tokens,
    norm_gain,
    window_weight,
    output_weight,
    token_slot,
    block_parcel,
    parcel_place,
    parcel_class,
    pool_exponent,
    embed_weight,
    parcel_gain,
    parcel_weight,
    merge_weight,
    adjacency,
):
    tile_rows, tile_cols, feature_width = tokens.shape
    row_count = lax.axis_size("tr")
    col_count = lax.axis_size("tc")
    row_index = lax.axis_index("tr")
    col_index = lax.axis_index("tc")
    tile_output = encode_tile(tokens, norm_gain, window_weight, output_weight)
    block_count = tile_rows * tile_cols // BLOCK
    feature_blocks = tile_output.reshape(block_count, BLOCK, feature_width)
    slot_blocks = token_slot.reshape(block_count, BLOCK)
    parcel_ids = block_parcel.reshape(block_count, KSLOT)
    live_slot = parcel_ids >= 0
    places = jnp.take(parcel_place, jnp.maximum(parcel_ids, 0))
    slot_class = jnp.take(parcel_class, places)
    class_match = slot_class[..., None] == jnp.arange(NCLASS, dtype=jnp.int32)
    slot_power = jnp.sum(jnp.where(class_match, pool_exponent, 0.0), axis=-1)
    onehot = (slot_blocks[..., None] == jnp.arange(KSLOT, dtype=jnp.int32)).astype(jnp.float32)
    token_power = jnp.sum(onehot * slot_power[:, None, :], axis=-1)
    lifted = jnp.exp(
        token_power[..., None]
        * jnp.log(jnp.maximum(feature_blocks.astype(jnp.float32), pool_floor))
    )
    block_sums = jnp.einsum(
        "bts,btd->bsd", onehot, lifted, precision=lax.Precision.HIGHEST
    ).reshape(-1, feature_width)
    block_counts = jnp.sum(onehot, axis=1).reshape(-1)
    devices = row_count * col_count
    capacity = 2 * (PARCELS_DEV // devices)
    slot_total = block_count * KSLOT
    flat_live = live_slot.reshape(-1)
    flat_place = places.reshape(-1)
    owner_device = jnp.where(flat_live, flat_place // PARCELS_DEV, devices)
    position = jnp.arange(slot_total, dtype=jnp.int32)
    earlier = (owner_device[None, :] == owner_device[:, None]) & (
        position[None, :] < position[:, None]
    )
    rank_within = jnp.sum(earlier, axis=1, dtype=jnp.int32)
    target = jnp.where(flat_live, owner_device * capacity + rank_within, devices * capacity)
    send_rows = (
        jnp.zeros((devices * capacity, feature_width), jnp.float32)
        .at[target]
        .set(block_sums, mode="drop")
    )
    send_counts = (
        jnp.zeros((devices * capacity,), jnp.float32).at[target].set(block_counts, mode="drop")
    )
    send_index = (
        jnp.full((devices * capacity,), -1.0, jnp.float32)
        .at[target]
        .set((flat_place % PARCELS_DEV).astype(jnp.float32), mode="drop")
    )
    received_rows, received_counts, received_index = (
        lax.all_to_all(
            send_rows.reshape(devices, capacity, feature_width).astype(jnp.bfloat16),
            ("tr", "tc"),
            split_axis=0,
            concat_axis=0,
            tiled=True,
        ).astype(jnp.float32),
        lax.all_to_all(
            send_counts.reshape(devices, capacity).astype(jnp.bfloat16),
            ("tr", "tc"),
            split_axis=0,
            concat_axis=0,
            tiled=True,
        ).astype(jnp.float32),
        lax.all_to_all(
            send_index.reshape(devices, capacity).astype(jnp.bfloat16),
            ("tr", "tc"),
            split_axis=0,
            concat_axis=0,
            tiled=True,
        ).astype(jnp.float32),
    )
    received_rows = received_rows.reshape(-1, feature_width)
    received_counts = received_counts.reshape(-1)
    received_index = received_index.reshape(-1)
    local_slot = jnp.where(received_index >= 0, received_index.astype(jnp.int32), PARCELS_DEV)
    power_sums = (
        jnp.zeros((PARCELS_DEV, feature_width), jnp.float32)
        .at[local_slot]
        .add(received_rows, mode="drop")
    )
    token_counts = (
        jnp.zeros((PARCELS_DEV,), jnp.float32).at[local_slot].add(received_counts, mode="drop")
    )
    device_index = row_index * col_count + col_index
    own_class = lax.dynamic_slice_in_dim(parcel_class, device_index * PARCELS_DEV, PARCELS_DEV)
    own_power = jnp.sum(
        jnp.where(own_class[:, None] == jnp.arange(NCLASS, dtype=jnp.int32), pool_exponent, 0.0),
        axis=-1,
    )
    pooled = jnp.exp(jnp.log(power_sums / token_counts[:, None]) / own_power[:, None]).astype(
        jnp.bfloat16
    )
    hidden_rows = jnp.dot(pooled, embed_weight, preferred_element_type=jnp.float32).astype(
        jnp.bfloat16
    )
    head_width = parcel_weight.shape[2]
    head_count = head_width // P_HDIM
    normed = layer_norm(
        lax.all_gather(hidden_rows, "tc", axis=0, tiled=True).astype(jnp.float32), parcel_gain
    ).astype(jnp.bfloat16)
    projected = jnp.einsum(
        "pd,kdh->pkh", normed, parcel_weight, preferred_element_type=jnp.float32
    ).astype(jnp.bfloat16)
    owner_total = projected.shape[0]
    owned_blocks = owner_total // PB
    pair_rows = jnp.concatenate([projected[:, 1], projected[:, 2]], axis=-1).reshape(
        owned_blocks, PB, 2 * head_width
    )
    neighbour_lists = adjacency.reshape(row_count, owned_blocks, NB)[:, :, 1:]
    own_blocks = row_index * owned_blocks + jnp.arange(owned_blocks, dtype=jnp.int32)
    wanted = jnp.any(
        neighbour_lists.reshape(row_count, -1)[:, :, None] == own_blocks[None, None, :], axis=1
    )
    wanted = wanted & (jnp.arange(row_count, dtype=jnp.int32) != row_index)[:, None]
    wanted_rank = jnp.cumsum(wanted.astype(jnp.int32), axis=1) - 1
    chooser = (
        wanted[:, None, :]
        & (wanted_rank[:, None, :] == jnp.arange(MAXB, dtype=jnp.int32)[None, :, None])
    ).astype(jnp.bfloat16)
    outgoing = jnp.einsum(
        "qsj,jpe->qspe", chooser, pair_rows, preferred_element_type=jnp.float32
    ).astype(jnp.bfloat16)
    incoming = lax.all_to_all(outgoing, "tr", split_axis=0, concat_axis=0, tiled=True)
    own_lists = lax.dynamic_index_in_dim(neighbour_lists, row_index, 0, keepdims=False)
    every_block = jnp.arange(row_count * owned_blocks, dtype=jnp.int32)
    needed = jnp.any(own_lists.reshape(-1)[None, :] == every_block[:, None], axis=1).reshape(
        row_count, owned_blocks
    )
    needed_rank = (jnp.cumsum(needed.astype(jnp.int32), axis=1) - 1).reshape(-1)
    source_row = own_lists // owned_blocks
    source_slot = jnp.take(needed_rank, own_lists)
    table_index = jnp.concatenate(
        [
            jnp.arange(owned_blocks, dtype=jnp.int32)[:, None],
            owned_blocks + source_row * MAXB + source_slot,
        ],
        axis=1,
    )
    pair_table = jnp.concatenate(
        [pair_rows, incoming.reshape(row_count * MAXB, PB, 2 * head_width)], axis=0
    )
    near_pairs = jnp.take(pair_table, table_index, axis=0).reshape(
        owned_blocks, NB * PB, 2, head_count, P_HDIM
    )
    query_blocks = projected[:, 0].reshape(owned_blocks, PB, head_count, P_HDIM)
    scores = jnp.einsum(
        "bqhd,bkhd->bhqk", query_blocks, near_pairs[:, :, 0], preferred_element_type=jnp.float32
    ) * P_HDIM ** (-0.5)
    weights = softmax_rows(scores).astype(jnp.bfloat16)
    attended = jnp.einsum(
        "bhqk,bkhd->bqhd", weights, near_pairs[:, :, 1], preferred_element_type=jnp.float32
    ).astype(jnp.bfloat16)
    attended = attended.reshape(owner_total, head_width)
    combined = lax.psum_scatter(
        jnp.dot(attended, merge_weight, preferred_element_type=jnp.float32).astype(jnp.bfloat16),
        "tc",
        scatter_dimension=0,
        tiled=True,
    ).astype(jnp.float32)
    parcel_vector = (combined + hidden_rows.astype(jnp.float32)).astype(jnp.bfloat16)
    return (tile_output, parcel_vector)


def solution(mesh):
    return jax.shard_map(
        body,
        mesh=mesh,
        in_specs=(
            P("tr", "tc", None),
            P(),
            P(),
            P(),
            P("tr", "tc"),
            P("tr", "tc", None),
            P(),
            P(),
            P(),
            P(),
            P(),
            P(None, None, "tc"),
            P("tc", None),
            P(),
        ),
        out_specs=(P("tr", "tc", None), P(("tr", "tc"), None)),
        check_vma=False,
    )
```

```python
import jax
import jax.numpy as jnp
from jax import lax
from jax.experimental import pallas as pl
from jax.experimental.pallas import tpu as pltpu
from jax.sharding import PartitionSpec as P

HEADS = 16
HDIM = 80
WIN = 8
SHIFT = 4
BLOCK = 128
KSLOT = 24
NCLASS = 8
PARCELS_DEV = 128
P_HDIM = 128
PB = 128
NB = 4
MAXB = 2


norm_epsilon = 1e-05
pool_floor = 1e-06


def layer_norm(values, norm_gain):
    centred = values - jnp.mean(values, axis=-1, keepdims=True)
    spread = jnp.mean(centred * centred, axis=-1, keepdims=True)
    return centred * lax.rsqrt(spread + norm_epsilon) * norm_gain


def softmax_rows(scores):
    row_top = jnp.max(scores, axis=-1, keepdims=True)
    lifted = jnp.exp(scores - row_top)
    return lifted / jnp.sum(lifted, axis=-1, keepdims=True)


MESH = pl.DeviceIdType.MESH
GROUP = 640
SUB = 16
DIRECTIONS = ((-1, -1), (-1, 0), (-1, 1), (0, -1), (0, 1), (1, -1), (1, 0), (1, 1))
SCALE = HDIM ** (-0.5) * 1.4426950408889634


def strip_perm(flip):
    first = lax.broadcasted_iota(jnp.int32, (BLOCK, BLOCK), 0)
    second = lax.broadcasted_iota(jnp.int32, (BLOCK, BLOCK), 1)
    out_at, in_at = (second, first) if flip else (first, second)
    source = ((out_at // 4) % 4) * 32 + (out_at // 16) * 4 + out_at % 4
    return jnp.where(source == in_at, 1.0, 0.0).astype(jnp.bfloat16)


def halo_part(step, width):
    if step == 0:
        return pl.ds(1, width), pl.ds(1, width)
    if step == 1:
        return pl.ds(width, 1), pl.ds(0, 1)
    return pl.ds(1, 1), pl.ds(width + 1, 1)


def window_pairs(qkv, group, key_at, query_at, out_at, mixed, bias):
    lane = lax.broadcasted_iota(jnp.int32, (1, 256), 1)
    low = lax.broadcasted_iota(jnp.int32, (1, 128), 1) < 64
    parts = [None] * 5
    sums = [None] * 5
    rows = query_at[2] * query_at[3] * SUB
    for pair in range(4):
        lanes = pl.ds(128 * pair, 256)
        query = qkv[group, pl.ds(query_at[0], query_at[2]), pl.ds(query_at[1], query_at[3]), :, lanes]
        query = query.reshape(rows, 256)
        keys = qkv[2 + group, pl.ds(key_at[0], 2), pl.ds(key_at[1], 2), :, lanes].reshape(64, 256)
        vals = qkv[4 + group, pl.ds(key_at[0], 2), pl.ds(key_at[1], 2), :, lanes].reshape(64, 256)
        start = 32 * pair
        even = (lane >= start) & (lane < start + HDIM)
        odd = (lane >= start + HDIM) & (lane < start + 2 * HDIM)
        zero = jnp.zeros((), jnp.bfloat16)
        both_keys = jnp.concatenate([jnp.where(even, keys, zero), jnp.where(odd, keys, zero)], axis=0)
        both_vals = jnp.concatenate([jnp.where(even, vals, zero), jnp.where(odd, vals, zero)], axis=0)
        ones = jnp.ones((64, 256), jnp.bfloat16)
        both_ones = jnp.concatenate([jnp.where(even, ones, zero), jnp.where(odd, ones, zero)], axis=0)
        scores = lax.dot_general(
            query, both_keys, (((1,), (1,)), ((), ())), preferred_element_type=jnp.float32
        )
        if bias is not None:
            scores = scores + bias
        top_low = jnp.max(jnp.where(low, scores, -jnp.inf), axis=-1, keepdims=True)
        top_high = jnp.max(jnp.where(low, -jnp.inf, scores), axis=-1, keepdims=True)
        lifted = jnp.exp2((scores - jnp.where(low, top_low, top_high)) * SCALE).astype(jnp.bfloat16)
        part = jnp.dot(lifted, both_vals, preferred_element_type=jnp.float32)
        total = jnp.dot(lifted, both_ones, preferred_element_type=jnp.float32)
        for half in range(2):
            at = pair + half
            cut = slice(128 * half, 128 * half + 128)
            parts[at] = part[:, cut] if parts[at] is None else parts[at] + part[:, cut]
            sums[at] = total[:, cut] if sums[at] is None else sums[at] + total[:, cut]
    for at in range(5):
        tile = (parts[at] / sums[at]).astype(jnp.bfloat16)
        mixed[group, pl.ds(out_at[0], query_at[2]), pl.ds(out_at[1], query_at[3]), :, pl.ds(128 * at, 128)] = (
            tile.reshape(query_at[2], query_at[3], SUB, 128)
        )


def window_kernel(
    tokens_hbm, gain_ref, packed_weight_hbm, out_weight_hbm, out_hbm,
    tokens, ext, qkv, mixed, packed_weight, out_weight,
    token_sem, weight_sem, out_sem, send_sem, recv_sem,
):
    row = lax.axis_index("tr")
    col = lax.axis_index("tc")
    n_row = lax.axis_size("tr")
    n_col = lax.axis_size("tc")

    def token_copy(strip):
        return pltpu.make_async_copy(tokens_hbm.at[strip], tokens.at[strip], token_sem.at[strip])

    def weight_copy(chunk):
        return pltpu.make_async_copy(
            packed_weight_hbm.at[:, pl.ds(pl.multiple_of(GROUP * chunk, 128), GROUP)],
            packed_weight.at[chunk],
            weight_sem.at[chunk],
        )

    out_weight_copy = pltpu.make_async_copy(out_weight_hbm, out_weight, weight_sem.at[6])

    def result_copy(strip):
        return pltpu.make_async_copy(tokens.at[strip], out_hbm.at[strip], out_sem.at[strip])

    for strip in range(8):
        token_copy(strip).start()
    for chunk in range(6):
        weight_copy(chunk).start()
    out_weight_copy.start()

    barrier = pltpu.get_barrier_semaphore()
    peers = [
        {"tr": lax.rem(row + dr + n_row, n_row), "tc": lax.rem(col + dc + n_col, n_col)}
        for dr, dc in DIRECTIONS
    ]
    for peer in peers:
        pl.semaphore_signal(barrier, inc=1, device_id=peer, device_id_type=MESH)

    forward = strip_perm(False)

    @pl.loop(0, 8)
    def _(strip):
        token_copy(strip).wait()
        values = jnp.dot(forward, tokens[strip], preferred_element_type=jnp.float32)
        normed = layer_norm(values, gain_ref[...]).astype(jnp.bfloat16)
        ext[strip + 1, pl.ds(1, 8)] = normed.reshape(8, SUB, 1280)

    pl.semaphore_wait(barrier, 8)
    copies = []
    for k, (dr, dc) in enumerate(DIRECTIONS):
        (from_row, to_row), (from_col, to_col) = halo_part(dr, 8), halo_part(dc, 8)
        copies.append(
            pltpu.make_async_remote_copy(
                src_ref=ext.at[from_row, from_col],
                dst_ref=ext.at[to_row, to_col],
                send_sem=send_sem.at[k],
                recv_sem=recv_sem.at[k],
                device_id=peers[k],
                device_id_type=MESH,
            )
        )
    for copy in copies:
        copy.start()

    @pl.loop(0, 6)
    def _(chunk):
        weight_copy(chunk).wait()

        @pl.loop(0, 2)
        def _(part):
            source = ext[pl.ds(1 + 4 * part, 4), pl.ds(1, 8)].reshape(512, 1280)
            packed = jnp.dot(source, packed_weight[chunk], preferred_element_type=jnp.float32)
            qkv[chunk, pl.ds(1 + 4 * part, 4), pl.ds(1, 8)] = packed.astype(jnp.bfloat16).reshape(4, 8, SUB, GROUP)

    for copy in copies:
        copy.wait_recv()

    @pl.loop(2, 6)
    def _(chunk):
        source = jnp.concatenate(
            [
                ext[0].reshape(160, 1280),
                ext[9].reshape(160, 1280),
                ext[pl.ds(1, 8), 0].reshape(128, 1280),
                ext[pl.ds(1, 8), 9].reshape(128, 1280),
            ],
            axis=0,
        )
        packed = jnp.dot(source, packed_weight[chunk], preferred_element_type=jnp.float32).astype(jnp.bfloat16)
        qkv[chunk, 0] = packed[0:160].reshape(10, SUB, GROUP)
        qkv[chunk, 9] = packed[160:320].reshape(10, SUB, GROUP)
        qkv[chunk, pl.ds(1, 8), 0] = packed[320:448].reshape(8, SUB, GROUP)
        qkv[chunk, pl.ds(1, 8), 9] = packed[448:576].reshape(8, SUB, GROUP)

    key_lane = lax.broadcasted_iota(jnp.int32, (1, 128), 1)
    upper = (key_lane // 32) % 2 == 0
    left = (key_lane // 16) % 2 == 0

    def bias_of(bad):
        return jnp.where(bad, -1e30, 0.0)

    @pl.loop(0, 2)
    def _(group):
        @pl.loop(0, 9)
        def _(window):
            a, b = window // 3 + 1, window % 3 + 1
            window_pairs(
                qkv, group, (2 * a, 2 * b), (2 * a, 2 * b, 2, 2), (2 * a - 1, 2 * b - 1), mixed, None
            )

        @pl.loop(0, 6)
        def _(window):
            side, b = window // 3, window % 3 + 1
            edge = ((side == 0) & (row == 0)) | ((side == 1) & (row == n_row - 1))
            bias = bias_of((upper == (side == 0)) & edge)
            window_pairs(
                qkv, group, (8 * side, 2 * b), (1 + 7 * side, 2 * b, 1, 2), (7 * side, 2 * b - 1), mixed, bias
            )

        @pl.loop(0, 6)
        def _(window):
            side, a = window // 3, window % 3 + 1
            edge = ((side == 0) & (col == 0)) | ((side == 1) & (col == n_col - 1))
            bias = bias_of((left == (side == 0)) & edge)
            window_pairs(
                qkv, group, (2 * a, 8 * side), (2 * a, 1 + 7 * side, 2, 1), (2 * a - 1, 7 * side), mixed, bias
            )

        @pl.loop(0, 4)
        def _(window):
            down, across = window // 2, window % 2
            edge_row = ((down == 0) & (row == 0)) | ((down == 1) & (row == n_row - 1))
            edge_col = ((across == 0) & (col == 0)) | ((across == 1) & (col == n_col - 1))
            bias = bias_of(((upper == (down == 0)) & edge_row) | ((left == (across == 0)) & edge_col))
            window_pairs(
                qkv, group, (8 * down, 8 * across), (1 + 7 * down, 1 + 7 * across, 1, 1),
                (7 * down, 7 * across), mixed, bias,
            )

    out_weight_copy.wait()
    backward = strip_perm(True)

    @pl.loop(0, 4)
    def _(part):
        sources = []
        for half in range(2):
            strip = 2 * part + half
            packed = jnp.concatenate(
                [mixed[0, strip].reshape(BLOCK, GROUP), mixed[1, strip].reshape(BLOCK, GROUP)], axis=1
            )
            sources.append(jnp.dot(backward, packed, preferred_element_type=jnp.float32).astype(jnp.bfloat16))
        layer_out = jnp.dot(
            jnp.concatenate(sources, axis=0), out_weight[...], preferred_element_type=jnp.float32
        )
        for half in range(2):
            strip = 2 * part + half
            tokens[strip] = (
                layer_out[BLOCK * half : BLOCK * half + BLOCK] + tokens[strip].astype(jnp.float32)
            ).astype(jnp.bfloat16)
            result_copy(strip).start()

    for strip in range(8):
        result_copy(strip).wait()
    for copy in copies:
        copy.wait_send()


def encode_tile(tokens, norm_gain, window_weight, output_weight):
    width = tokens.shape[2]
    anywhere = pl.BlockSpec(memory_space=pl.ANY)
    inside = pl.BlockSpec(memory_space=pltpu.VMEM)
    bf16 = jnp.bfloat16
    out = pl.pallas_call(
        window_kernel,
        out_shape=jax.ShapeDtypeStruct((8, BLOCK, width), bf16),
        in_specs=[anywhere, inside, anywhere, anywhere],
        out_specs=anywhere,
        scratch_shapes=[
            pltpu.VMEM((8, BLOCK, width), bf16),
            pltpu.VMEM((10, 10, SUB, width), bf16),
            pltpu.VMEM((6, 10, 10, SUB, GROUP), bf16),
            pltpu.VMEM((2, 8, 8, SUB, GROUP), bf16),
            pltpu.VMEM((6, width, GROUP), bf16),
            pltpu.VMEM((width, width), bf16),
            pltpu.SemaphoreType.DMA((8,)),
            pltpu.SemaphoreType.DMA((7,)),
            pltpu.SemaphoreType.DMA((8,)),
            pltpu.SemaphoreType.DMA((8,)),
            pltpu.SemaphoreType.DMA((8,)),
        ],
        compiler_params=pltpu.CompilerParams(
            collective_id=1, has_side_effects=True, vmem_limit_bytes=58 * 1024 * 1024
        ),
        cost_estimate=pl.CostEstimate(flops=20 * 10**9, bytes_accessed=20 * 10**6, transcendentals=2 * 10**6),
        name="window_attention",
    )(tokens.reshape(8, BLOCK, width), norm_gain.reshape(1, width), window_weight, output_weight)
    return out


META = 128


def onto_rows(column, size):
    here = lax.broadcasted_iota(jnp.int32, (size, size), 0) == lax.broadcasted_iota(jnp.int32, (size, size), 1)
    return jnp.sum(jnp.where(here, column, 0.0), axis=0, keepdims=True)


def onto_columns(row, size):
    here = lax.broadcasted_iota(jnp.int32, (size, size), 0) == lax.broadcasted_iota(jnp.int32, (size, size), 1)
    return jnp.sum(jnp.where(here, row, 0.0), axis=1, keepdims=True)


def exponent_of(kind, exponents):
    power = jnp.zeros_like(kind)
    for k in range(NCLASS):
        power = jnp.where(kind == k, exponents[k], power)
    return power


def picked(select, at, table):
    lane = lax.broadcasted_iota(jnp.int32, (select.shape[0], 128), 1).astype(jnp.float32)
    rows = jnp.dot(
        (select == lane).astype(jnp.bfloat16), table.astype(jnp.bfloat16), preferred_element_type=jnp.float32
    )
    return jnp.sum(jnp.where(at == lane, rows, 0.0), axis=1, keepdims=True)


def meet(peers, own):
    barrier = pltpu.get_barrier_semaphore()
    for peer in peers:
        pl.semaphore_signal(barrier, inc=1, device_id=peer, device_id_type=MESH)
    own()
    pl.semaphore_wait(barrier, len(peers))


def peers_of(row, col, n_row, n_col):
    down = [{"tr": lax.rem(row + k, n_row), "tc": col} for k in range(1, n_row)]
    across = [{"tr": row, "tc": lax.rem(col + k, n_col)} for k in range(1, n_col)]
    return down, across


def exchange(axis, index, peers, source, target, send_sem, recv_sem):
    copies = []
    for k, peer in enumerate(peers):
        copies.append(
            pltpu.make_async_remote_copy(
                src_ref=source.at[peer[axis]],
                dst_ref=target.at[index],
                send_sem=send_sem.at[k],
                recv_sem=recv_sem.at[k],
                device_id=peer,
                device_id_type=MESH,
            )
        )
    for copy in copies:
        copy.start()
    return copies


def pool_kernel(
    tile_ref, slot_ref, parcel_ref, place_ref, class_ref, exponents, embed_hbm, gain_ref,
    hidden_ref, normed_ref,
    embed, sums, send_a, recv_a, send_b, recv_b,
    embed_sem, send_sem_a, recv_sem_a, send_sem_b, recv_sem_b,
):
    row = lax.axis_index("tr")
    col = lax.axis_index("tc")
    n_row = lax.axis_size("tr")
    n_col = lax.axis_size("tc")
    width = tile_ref.shape[2]
    embed_copy = pltpu.make_async_copy(embed_hbm, embed, embed_sem)
    embed_copy.start()
    down, across = peers_of(row, col, n_row, n_col)
    slots = 8 * KSLOT

    def pool():
        ids = jnp.concatenate(
            [jnp.broadcast_to(parcel_ref[u : u + 1, :], (KSLOT, KSLOT)) for u in range(8)], axis=0
        )
        at = lax.broadcasted_iota(jnp.int32, (slots, KSLOT), 1) == lax.rem(
            lax.broadcasted_iota(jnp.int32, (slots, KSLOT), 0), KSLOT
        )
        ids = jnp.sum(jnp.where(at, ids.astype(jnp.float32), 0.0), axis=1, keepdims=True)
        live = ids >= 0
        ids = jnp.maximum(ids, 0.0)
        ids_high = jnp.floor(ids * (1.0 / 128.0))
        ids_low = ids - ids_high * 128.0
        place = place_ref[...]
        owner = picked(ids_high, ids_low, (place // 128).astype(jnp.float32))
        local = picked(ids_high, ids_low, (place % 128).astype(jnp.float32))
        kind = picked(owner, local, class_ref[...].astype(jnp.float32))
        power = exponent_of(kind, exponents)
        owner = jnp.where(live, owner, -1.0)
        owner_row = onto_rows(owner, slots)
        earlier = lax.broadcasted_iota(jnp.int32, (slots, slots), 1) < lax.broadcasted_iota(
            jnp.int32, (slots, slots), 0
        )
        rank = jnp.sum(jnp.where((owner == owner_row) & earlier, 1.0, 0.0), axis=1, keepdims=True)
        target = jnp.where(live, owner * 2.0 + rank, -1.0)
        target_row = onto_rows(target, slots)
        lane = lax.broadcasted_iota(jnp.int32, (KSLOT, META), 1)
        for strip in range(8):
            cut = slice(KSLOT * strip, KSLOT * strip + KSLOT)
            match = (
                lax.broadcasted_iota(jnp.int32, (KSLOT, BLOCK), 0) == slot_ref[strip : strip + 1, :]
            ).astype(jnp.float32)
            token_power = onto_columns(jnp.sum(match * power[cut], axis=0, keepdims=True), BLOCK)
            values = jnp.maximum(tile_ref[strip].astype(jnp.float32), pool_floor)
            lifted = jnp.exp(token_power * jnp.log(values))
            sums[cut, 0:width] = jnp.dot(
                match.astype(jnp.bfloat16), lifted.astype(jnp.bfloat16), preferred_element_type=jnp.float32
            )
            count = jnp.sum(match, axis=1, keepdims=True)
            sums[cut, width : width + META] = jnp.where(
                lane == 0, count, jnp.where(lane == 1, local[cut], 0.0)
            )
        chooser = (
            lax.broadcasted_iota(jnp.int32, (256, slots), 0).astype(jnp.float32) == target_row
        ).astype(jnp.bfloat16)
        rows = jnp.dot(chooser, sums[...].astype(jnp.bfloat16), preferred_element_type=jnp.float32)
        send_a[...] = rows.astype(jnp.bfloat16).reshape(16, 16, width + META)

    meet(down + across, pool)
    copies_a = exchange("tr", row, down, send_a, recv_a, send_sem_a, recv_sem_a)
    recv_a[row] = send_a[row]
    for copy in copies_a:
        copy.wait_recv()
    out_at = lax.broadcasted_iota(jnp.int32, (256, 256), 0)
    in_at = lax.broadcasted_iota(jnp.int32, (256, 256), 1)
    swap = jnp.where(((out_at // 2) % 16) * 16 + (out_at // 32) * 2 + out_at % 2 == in_at, 1.0, 0.0)
    rows = jnp.dot(
        swap.astype(jnp.bfloat16), recv_a[...].reshape(256, width + META), preferred_element_type=jnp.float32
    )
    send_b[...] = rows.astype(jnp.bfloat16).reshape(8, 32, width + META)
    copies_b = exchange("tc", col, across, send_b, recv_b, send_sem_b, recv_sem_b)
    recv_b[col] = send_b[col]
    own_kind = class_ref[pl.ds(row * n_col + col, 1), :].astype(jnp.float32)
    own_power = onto_columns(exponent_of(own_kind, exponents), PARCELS_DEV)
    for copy in copies_b:
        copy.wait_recv()
    arrived = recv_b[...].reshape(256, width + META)
    info = arrived[:, width : width + META].astype(jnp.float32)
    count, local = info[:, 0:1], info[:, 1:2]
    lane = lax.broadcasted_iota(jnp.int32, (256, PARCELS_DEV), 1).astype(jnp.float32)
    placed = jnp.where((lane == local) & (count > 0), 1.0, 0.0).astype(jnp.bfloat16)
    total = lax.dot_general(placed, arrived, (((0,), (0,)), ((), ())), preferred_element_type=jnp.float32)
    power_sums, counts = total[:, 0:width], total[:, width : width + 1]
    pooled = jnp.exp(jnp.log(power_sums / counts) / own_power).astype(jnp.bfloat16)
    embed_copy.wait()
    hidden = jnp.dot(pooled, embed[...], preferred_element_type=jnp.float32).astype(jnp.bfloat16)
    hidden_ref[...] = hidden
    normed_ref[...] = layer_norm(hidden.astype(jnp.float32), gain_ref[...]).astype(jnp.bfloat16)
    for copy in copies_a + copies_b:
        copy.wait_send()


def pool_parcels(tile, slots, parcels, places, kinds, exponents, embed_weight, parcel_gain):
    width = tile.shape[2]
    rows_out = embed_weight.shape[1]
    inside = pl.BlockSpec(memory_space=pltpu.VMEM)
    bf16 = jnp.bfloat16
    out = jax.ShapeDtypeStruct((PARCELS_DEV, rows_out), bf16)
    return pl.pallas_call(
        pool_kernel,
        out_shape=(out, out),
        in_specs=[
            inside, inside, inside, inside, inside,
            pl.BlockSpec(memory_space=pltpu.SMEM),
            pl.BlockSpec(memory_space=pl.ANY),
            inside,
        ],
        out_specs=(inside, inside),
        scratch_shapes=[
            pltpu.VMEM((width, rows_out), bf16),
            pltpu.VMEM((8 * KSLOT, width + META), jnp.float32),
            pltpu.VMEM((16, 16, width + META), bf16),
            pltpu.VMEM((16, 16, width + META), bf16),
            pltpu.VMEM((8, 32, width + META), bf16),
            pltpu.VMEM((8, 32, width + META), bf16),
            pltpu.SemaphoreType.DMA,
            pltpu.SemaphoreType.DMA((15,)),
            pltpu.SemaphoreType.DMA((15,)),
            pltpu.SemaphoreType.DMA((7,)),
            pltpu.SemaphoreType.DMA((7,)),
        ],
        compiler_params=pltpu.CompilerParams(
            collective_id=2, has_side_effects=True, vmem_limit_bytes=40 * 1024 * 1024
        ),
        cost_estimate=pl.CostEstimate(flops=10**9, bytes_accessed=10**7, transcendentals=3 * 10**6),
        name="parcel_pooling",
    )(tile, slots, parcels, places, kinds, exponents, embed_weight, parcel_gain.reshape(1, rows_out))


def parcel_kernel(
    pick_out, pick_in, normed_ref, hidden_ref, weight_hbm, merge_hbm, out_ref,
    weight, merge, send_1, recv_1, send_2, recv_2, send_3, recv_3, near, keys, vals,
    weight_sem, send_sem_1, recv_sem_1, send_sem_2, recv_sem_2, send_sem_3, recv_sem_3,
):
    row = lax.axis_index("tr")
    col = lax.axis_index("tc")
    n_row = lax.axis_size("tr")
    n_col = lax.axis_size("tc")
    down, across = peers_of(row, col, n_row, n_col)
    weight_copies = [
        pltpu.make_async_copy(
            weight_hbm.at[head, third], weight.at[third, :, pl.ds(P_HDIM * head, P_HDIM)], weight_sem.at[third, head]
        )
        for third in range(3)
        for head in range(8)
    ]
    merge_copy = pltpu.make_async_copy(merge_hbm, merge, weight_sem.at[3, 0])
    for copy in weight_copies:
        copy.start()
    merge_copy.start()

    def own():
        for part in range(8):
            send_1[part] = normed_ref[:, P_HDIM * part : P_HDIM * part + P_HDIM]

    meet(down + across, own)
    copies_1 = exchange("tc", col, across, send_1, recv_1, send_sem_1, recv_sem_1)
    recv_1[col] = send_1[col]
    for copy in copies_1:
        copy.wait_recv()
    copies_2 = []
    for k, peer in enumerate(down):
        there = peer["tr"]
        for slot in range(MAXB):
            send_2[there, slot] = recv_1[pick_out[there, slot]]
    copies_2 = exchange("tr", row, down, send_2, recv_2, send_sem_2, recv_sem_2)
    recv_2[row] = jnp.zeros((MAXB, PB, P_HDIM), jnp.bfloat16)

    for copy in weight_copies:
        copy.wait()
    normed = normed_ref[...]
    query = jnp.dot(normed, weight[0], preferred_element_type=jnp.float32).astype(jnp.bfloat16)
    keys[0:PB] = jnp.dot(normed, weight[1], preferred_element_type=jnp.float32).astype(jnp.bfloat16)
    vals[0:PB] = jnp.dot(normed, weight[2], preferred_element_type=jnp.float32).astype(jnp.bfloat16)

    for copy in copies_2:
        copy.wait_recv()
    for there in range(8):
        for j in range(NB - 1):
            at = pick_in[there, j]
            send_3[there, j] = recv_2[at // MAXB, at % MAXB]
    copies_3 = exchange("tc", col, across, send_3, recv_3, send_sem_3, recv_sem_3)
    recv_3[col] = send_3[col]
    for copy in copies_3:
        copy.wait_recv()
    for part in range(8):
        near[:, P_HDIM * part : P_HDIM * part + P_HDIM] = recv_3[part].reshape((NB - 1) * PB, P_HDIM)
    keys[PB:] = jnp.dot(near[...], weight[1], preferred_element_type=jnp.float32).astype(jnp.bfloat16)
    vals[PB:] = jnp.dot(near[...], weight[2], preferred_element_type=jnp.float32).astype(jnp.bfloat16)
    attended = []
    for head in range(8):
        cut = slice(P_HDIM * head, P_HDIM * head + P_HDIM)
        scores = lax.dot_general(
            query[:, cut], keys[:, cut], (((1,), (1,)), ((), ())), preferred_element_type=jnp.float32
        ) * P_HDIM ** (-0.5)
        weights = softmax_rows(scores).astype(jnp.bfloat16)
        attended.append(
            jnp.dot(weights, vals[:, cut], preferred_element_type=jnp.float32).astype(jnp.bfloat16)
        )
    merge_copy.wait()
    combined = jnp.dot(
        jnp.concatenate(attended, axis=1), merge[...], preferred_element_type=jnp.float32
    )
    out_ref[...] = (combined + hidden_ref[...].astype(jnp.float32)).astype(jnp.bfloat16)
    for copy in copies_1 + copies_2 + copies_3:
        copy.wait_send()


def parcel_attention(pick_out, pick_in, normed, hidden, weight, merge):
    bf16 = jnp.bfloat16
    inside = pl.BlockSpec(memory_space=pltpu.VMEM)
    scalars = pl.BlockSpec(memory_space=pltpu.SMEM)
    anywhere = pl.BlockSpec(memory_space=pl.ANY)
    rows, width = normed.shape
    return pl.pallas_call(
        parcel_kernel,
        out_shape=jax.ShapeDtypeStruct((rows, width), bf16),
        in_specs=[scalars, scalars, inside, inside, anywhere, anywhere],
        out_specs=inside,
        scratch_shapes=[
            pltpu.VMEM((3, width, width), bf16),
            pltpu.VMEM((width, width), bf16),
            pltpu.VMEM((8, PB, P_HDIM), bf16),
            pltpu.VMEM((8, PB, P_HDIM), bf16),
            pltpu.VMEM((16, MAXB, PB, P_HDIM), bf16),
            pltpu.VMEM((16, MAXB, PB, P_HDIM), bf16),
            pltpu.VMEM((8, NB - 1, PB, P_HDIM), bf16),
            pltpu.VMEM((8, NB - 1, PB, P_HDIM), bf16),
            pltpu.VMEM(((NB - 1) * PB, width), bf16),
            pltpu.VMEM((NB * PB, width), bf16),
            pltpu.VMEM((NB * PB, width), bf16),
            pltpu.SemaphoreType.DMA((4, 8)),
            pltpu.SemaphoreType.DMA((7,)),
            pltpu.SemaphoreType.DMA((7,)),
            pltpu.SemaphoreType.DMA((15,)),
            pltpu.SemaphoreType.DMA((15,)),
            pltpu.SemaphoreType.DMA((7,)),
            pltpu.SemaphoreType.DMA((7,)),
        ],
        compiler_params=pltpu.CompilerParams(
            collective_id=3, has_side_effects=True, vmem_limit_bytes=48 * 1024 * 1024
        ),
        cost_estimate=pl.CostEstimate(flops=3 * 10**9, bytes_accessed=10**7, transcendentals=10**6),
        name="parcel_attention",
    )(pick_out, pick_in, normed, hidden, weight, merge)


def exchange_lists(adjacency, row_index, row_count):
    owned = adjacency.shape[0] // row_count
    lists = adjacency.reshape(row_count, owned, NB)[:, :, 1:].reshape(row_count, owned * (NB - 1))
    blocks = jnp.arange(row_count * owned, dtype=jnp.int32)
    needed = jnp.any(lists[:, :, None] == blocks[None, None, :], axis=1).reshape(row_count, row_count, owned)
    inner = jnp.arange(owned, dtype=jnp.int32)
    rank = jnp.sum(
        needed[:, :, None, :] & (inner[None, :] < inner[:, None])[None, None], axis=-1, dtype=jnp.int32
    )
    asked = lax.dynamic_index_in_dim(needed, row_index, 1, keepdims=False)
    asked_rank = lax.dynamic_index_in_dim(rank, row_index, 1, keepdims=False)
    slot = jnp.arange(MAXB, dtype=jnp.int32)
    pick_out = jnp.sum(
        jnp.where(asked[:, None, :] & (asked_rank[:, None, :] == slot[None, :, None]), inner, 0), axis=-1
    )
    own_list = lax.dynamic_index_in_dim(lists, row_index, 0, keepdims=False)
    own_rank = lax.dynamic_index_in_dim(rank, row_index, 0, keepdims=False).reshape(-1)
    place = (blocks // owned) * MAXB + own_rank
    pick_in = jnp.sum(jnp.where(own_list[:, None] == blocks[None, :], place[None, :], 0), axis=1)
    return pick_out.astype(jnp.int32), pick_in.astype(jnp.int32).reshape(owned, NB - 1)


def body(
    tokens,
    norm_gain,
    window_weight,
    output_weight,
    token_slot,
    block_parcel,
    parcel_place,
    parcel_class,
    pool_exponent,
    embed_weight,
    parcel_gain,
    parcel_weight,
    merge_weight,
    adjacency,
):
    row_index = lax.axis_index("tr")
    row_count = lax.axis_size("tr")
    weight = lax.all_gather(parcel_weight, "tc", axis=0, tiled=False)
    merge = lax.all_gather(merge_weight, "tc", axis=0, tiled=True)
    pick_out, pick_in = exchange_lists(adjacency, row_index, row_count)
    tile = encode_tile(tokens, norm_gain, window_weight, output_weight)
    hidden, normed = pool_parcels(
        tile,
        token_slot.reshape(8, BLOCK),
        block_parcel.reshape(8, KSLOT),
        parcel_place.reshape(128, 128),
        parcel_class.reshape(128, 128),
        pool_exponent,
        embed_weight,
        parcel_gain,
    )
    parcel_vector = parcel_attention(pick_out, pick_in, normed, hidden, weight, merge)
    return (tile.reshape(tokens.shape), parcel_vector)


def solution(mesh):
    return jax.shard_map(
        body,
        mesh=mesh,
        in_specs=(
            P("tr", "tc", None),
            P(),
            P(),
            P(),
            P("tr", "tc"),
            P("tr", "tc", None),
            P(),
            P(),
            P(),
            P(),
            P(),
            P(None, None, "tc"),
            P("tc", None),
            P(),
        ),
        out_specs=(P("tr", "tc", None), P(("tr", "tc"), None)),
        check_vma=False,
    )
```

```python
import jax
import jax.numpy as jnp
from jax import lax
from jax.experimental import pallas as pl
from jax.experimental.pallas import tpu as pltpu
from jax.sharding import PartitionSpec as P

HEADS = 16
HDIM = 80
BLOCK = 128
KSLOT = 24
NCLASS = 8
PARCELS_DEV = 128
P_HDIM = 128
PB = 128
NB = 4
MAXB = 2


norm_epsilon = 1e-05
pool_floor = 1e-06


def layer_norm(values, norm_gain):
    centred = values - jnp.mean(values, axis=-1, keepdims=True)
    spread = jnp.mean(centred * centred, axis=-1, keepdims=True)
    return centred * lax.rsqrt(spread + norm_epsilon) * norm_gain


def softmax_rows(scores):
    row_top = jnp.max(scores, axis=-1, keepdims=True)
    lifted = jnp.exp(scores - row_top)
    return lifted / jnp.sum(lifted, axis=-1, keepdims=True)


MESH = pl.DeviceIdType.MESH
GROUP = 640
SUB = 16
SCALE = HDIM ** (-0.5) * 1.4426950408889634


def strip_perm(flip):
    first = lax.broadcasted_iota(jnp.int32, (BLOCK, BLOCK), 0)
    second = lax.broadcasted_iota(jnp.int32, (BLOCK, BLOCK), 1)
    out_at, in_at = (second, first) if flip else (first, second)
    source = ((out_at // 4) % 4) * 32 + (out_at // 16) * 4 + out_at % 4
    return jnp.where(source == in_at, 1.0, 0.0).astype(jnp.bfloat16)


def window_pairs(qkv, group, at, mixed, bias):
    lane = lax.broadcasted_iota(jnp.int32, (1, 256), 1)
    low = lax.broadcasted_iota(jnp.int32, (1, 128), 1) < 64
    zero = jnp.zeros((), jnp.bfloat16)
    halves = (
        lax.broadcasted_iota(jnp.int32, (128, 128), 0) // 64 == lax.broadcasted_iota(jnp.int32, (128, 128), 1) // 64
    )
    halves = jnp.where(halves, 1.0, 0.0).astype(jnp.bfloat16)

    def part_of(third, pair):
        lanes = pl.ds(128 * pair, 256)
        return qkv[2 * third + group, pl.ds(at[0], 2), pl.ds(at[1], 2), :, lanes].reshape(64, 256)

    def split(values, pair):
        start = 32 * pair
        even = (lane >= start) & (lane < start + HDIM)
        odd = (lane >= start + HDIM) & (lane < start + 2 * HDIM)
        return jnp.concatenate([jnp.where(even, values, zero), jnp.where(odd, values, zero)], axis=0)

    lifted = []
    for pair in range(4):
        scores = lax.dot_general(
            part_of(0, pair), split(part_of(1, pair), pair), (((1,), (1,)), ((), ())),
            preferred_element_type=jnp.float32,
        )
        if bias is not None:
            scores = scores + bias
        top_low = jnp.max(jnp.where(low, scores, -jnp.inf), axis=-1, keepdims=True)
        top_high = jnp.max(jnp.where(low, -jnp.inf, scores), axis=-1, keepdims=True)
        lifted.append(jnp.exp2((scores - jnp.where(low, top_low, top_high)) * SCALE))
    lifted = jnp.concatenate(lifted, axis=0)
    total = jnp.dot(lifted.astype(jnp.bfloat16), halves, preferred_element_type=jnp.float32)
    weights = (lifted / total).astype(jnp.bfloat16)
    parts = [None] * 5
    for pair in range(4):
        part = jnp.dot(
            weights[64 * pair : 64 * pair + 64], split(part_of(2, pair), pair), preferred_element_type=jnp.float32
        )
        for half in range(2):
            cut = part[:, 128 * half : 128 * half + 128]
            parts[pair + half] = cut if parts[pair + half] is None else parts[pair + half] + cut
    for tile in range(5):
        mixed[group, pl.ds(at[0], 2), pl.ds(at[1], 2), :, pl.ds(128 * tile, 128)] = (
            parts[tile].astype(jnp.bfloat16).reshape(2, 2, SUB, 128)
        )


META = 128
PIECES = 2
PIECE = PB // PIECES


def onto_rows(column, size):
    here = lax.broadcasted_iota(jnp.int32, (size, size), 0) == lax.broadcasted_iota(jnp.int32, (size, size), 1)
    return jnp.sum(jnp.where(here, column, 0.0), axis=0, keepdims=True)


def onto_columns(row, size):
    here = lax.broadcasted_iota(jnp.int32, (size, size), 0) == lax.broadcasted_iota(jnp.int32, (size, size), 1)
    return jnp.sum(jnp.where(here, row, 0.0), axis=1, keepdims=True)


def exponent_of(kind, exponents):
    power = jnp.zeros_like(kind)
    for k in range(NCLASS):
        power = jnp.where(kind == k, exponents[k], power)
    return power


def picked(select, at, table):
    lane = lax.broadcasted_iota(jnp.int32, (select.shape[0], 128), 1).astype(jnp.float32)
    rows = jnp.dot(
        (select == lane).astype(jnp.bfloat16), table.astype(jnp.bfloat16), preferred_element_type=jnp.float32
    )
    return jnp.sum(jnp.where(at == lane, rows, 0.0), axis=1, keepdims=True)


def exchange(axis, index, peers, source, target, send_sem, recv_sem):
    copies = []
    for k, peer in enumerate(peers):
        copies.append(
            pltpu.make_async_remote_copy(
                src_ref=source.at[peer[axis]],
                dst_ref=target.at[index],
                send_sem=send_sem.at[k],
                recv_sem=recv_sem.at[k],
                device_id=peer,
                device_id_type=MESH,
            )
        )
    for copy in copies:
        copy.start()
    return copies


def whole_kernel(
    tokens_hbm, gain_ref, packed_weight_hbm, out_weight_hbm, parcel_weight_hbm, merge_hbm,
    slot_ref, parcel_ref, place_ref, class_ref, exponents, embed_hbm, parcel_gain, adjacency,
    out_hbm, out_ref,
    tokens, region, qkv, mixed, packed_weight, out_weight, weight, merge, embed, sums,
    send_a0, send_a1, recv_a0, recv_a1, send_b0, send_b1, recv_b0, recv_b1,
    send_1, send_2, send_3, recv_3, keys, vals, pick_out, pick_in, recv_1_0, recv_1_1, recv_2_0, recv_2_1,
    token_sem, weight_sem, out_sem, halo_send, halo_recv, back_send, back_recv,
    keep_sem, first_send, first_recv, second_send, second_recv, twin_send, twin_recv,
    send_sem_a, recv_sem_a, send_sem_b, recv_sem_b,
    send_sem_1, recv_sem_1, send_sem_2, recv_sem_2, send_sem_3, recv_sem_3,
):
    row = lax.axis_index("tr")
    col = lax.axis_index("tc")
    n_row = lax.axis_size("tr")
    n_col = lax.axis_size("tc")

    def token_copy(strip):
        return pltpu.make_async_copy(tokens_hbm.at[strip], tokens.at[strip], token_sem.at[strip])

    def weight_copy(chunk):
        return pltpu.make_async_copy(
            packed_weight_hbm.at[:, pl.ds(pl.multiple_of(GROUP * chunk, 128), GROUP)],
            packed_weight.at[chunk],
            weight_sem.at[chunk],
        )

    out_weight_copy = pltpu.make_async_copy(out_weight_hbm, out_weight, weight_sem.at[6])

    def result_copy(strip):
        return pltpu.make_async_copy(tokens.at[strip], out_hbm.at[strip], out_sem.at[strip])

    def remote(source, target, send, recv, peer):
        return pltpu.make_async_remote_copy(
            src_ref=source, dst_ref=target, send_sem=send, recv_sem=recv, device_id=peer, device_id_type=MESH
        )

    for strip in range(8):
        token_copy(strip).start()
    for chunk in range(6):
        weight_copy(chunk).start()
    out_weight_copy.start()
    embed_copy = pltpu.make_async_copy(embed_hbm, embed, weight_sem.at[7])
    embed_copy.start()

    def peer_at(dr, dc):
        return {"tr": lax.rem(row + dr + n_row, n_row), "tc": lax.rem(col + dc + n_col, n_col)}

    x, z = lax.rem(row, 4), row // 4
    ahead = [peer_at(1, 0), peer_at(0, 1), peer_at(1, 1)]
    behind = [peer_at(-1, 0), peer_at(0, -1), peer_at(-1, -1)]
    along_y = [peer_at(0, 2 * k) for k in range(1, 4)]
    along_x = [{"tr": z * 4 + lax.rem(x + k, 4), "tc": col} for k in range(1, 4)]
    along_z = [{"tr": lax.rem(z + k, 4) * 4 + x, "tc": col} for k in range(1, 4)]
    down = [peer_at(k, 0) for k in range(1, n_row)]
    across = [peer_at(0, k) for k in range(1, n_col)]
    peers = down + across + [ahead[2], behind[2]]
    barrier = pltpu.get_barrier_semaphore()
    for peer in peers:
        pl.semaphore_signal(barrier, inc=1, device_id=peer, device_id_type=MESH)

    forward = strip_perm(False)

    @pl.loop(0, 8)
    def _(strip):
        token_copy(strip).wait()
        values = jnp.dot(forward, tokens[strip], preferred_element_type=jnp.float32)
        normed = layer_norm(values, gain_ref[...].reshape(1, 1280)).astype(jnp.bfloat16)
        region[strip + 1, pl.ds(1, 8)] = normed.reshape(8, SUB, 1280)

    pl.semaphore_wait(barrier, len(peers))
    inner = pl.ds(1, 7)
    halo = [
        remote(region.at[8, inner], region.at[0, inner], halo_send.at[0], halo_recv.at[0], ahead[0]),
        remote(region.at[inner, 8], region.at[inner, 0], halo_send.at[1], halo_recv.at[1], ahead[1]),
        remote(region.at[8, 8], region.at[0, 0], halo_send.at[2], halo_recv.at[2], ahead[2]),
    ]
    x_rows = pl.ds(pl.multiple_of(256 * x, 256), 256)

    def lanes_of(head):
        return pl.ds(pl.multiple_of(P_HDIM * head, P_HDIM), P_HDIM)

    def merge_rows(head):
        return pl.ds(pl.multiple_of(P_HDIM * head + 32 * z, 32), 32)

    own = lanes_of(col)
    keep = [
        pltpu.make_async_copy(parcel_weight_hbm, weight.at[:, :, own], keep_sem.at[0]),
        pltpu.make_async_copy(merge_hbm, merge.at[own], keep_sem.at[1]),
    ]
    quarters, wholes, relays, twins = [], [], [], []
    twin = {"tr": row, "tc": col + 1 - 2 * lax.rem(col, 2)}
    for k, peer in enumerate(along_y):
        quarters.append(
            remote(
                parcel_weight_hbm.at[0, x_rows], weight.at[0, x_rows, own],
                first_send.at[0, k], first_recv.at[0, k], peer,
            )
        )
        quarters.append(
            remote(
                merge_hbm.at[pl.ds(pl.multiple_of(32 * z, 32), 32)], merge.at[merge_rows(col)],
                first_send.at[1, k], first_recv.at[1, k], peer,
            )
        )
        wholes.append(
            remote(
                parcel_weight_hbm.at[pl.ds(1, 2)], weight.at[pl.ds(1, 2), :, own],
                first_send.at[2, k], first_recv.at[2, k], peer,
            )
        )
        there = lax.rem(col + 2 * (k + 1), n_col)
        for j in range(3):
            q_part = weight.at[0, x_rows, lanes_of(there)]
            relays.append(remote(q_part, q_part, second_send.at[0, k, j], second_recv.at[0, k, j], along_x[j]))
            merge_part = merge.at[merge_rows(there)]
            relays.append(
                remote(merge_part, merge_part, second_send.at[1, k, j], second_recv.at[1, k, j], along_z[j])
            )
    for k in range(4):
        there = lanes_of(lax.rem(col + 2 * k, n_col))
        for j, part in enumerate((weight.at[:, :, there], merge.at[there])):
            twins.append(remote(part, part, twin_send.at[j, k], twin_recv.at[j, k], twin))
    for copy in halo + quarters + wholes + keep:
        copy.start()

    @pl.loop(0, 6)
    def _(chunk):
        weight_copy(chunk).wait()
        source = region[inner, inner].reshape(784, 1280)
        packed = jnp.dot(source, packed_weight[chunk], preferred_element_type=jnp.float32)
        qkv[chunk, inner, inner] = packed.astype(jnp.bfloat16).reshape(7, 7, SUB, GROUP)

    for copy in quarters:
        copy.wait_recv()
    for copy in relays:
        copy.start()
    for copy in halo:
        copy.wait_recv()

    @pl.loop(0, 6)
    def _(chunk):
        source = jnp.concatenate(
            [region[0, pl.ds(0, 8)].reshape(128, 1280), region[inner, 0].reshape(112, 1280)], axis=0
        )
        packed = jnp.dot(source, packed_weight[chunk], preferred_element_type=jnp.float32).astype(jnp.bfloat16)
        qkv[chunk, 0] = packed[0:128].reshape(8, SUB, GROUP)
        qkv[chunk, inner, 0] = packed[128:240].reshape(7, SUB, GROUP)

    key_at = lax.broadcasted_iota(jnp.int32, (64, 128), 1) % 64
    query_at = lax.broadcasted_iota(jnp.int32, (64, 128), 0)
    row_cut = (key_at // 32 != query_at // 32) & (row == 0)
    col_cut = ((key_at // 16) % 2 != (query_at // 16) % 2) & (col == 0)

    def bias_of(cut):
        return jnp.where(cut, -1e30, 0.0)

    for group in range(2):
        window_pairs(qkv, group, (0, 0), mixed, bias_of(row_cut | col_cut))

    @pl.loop(1, 4)
    def _(a):
        for group in range(2):
            window_pairs(qkv, group, (0, 2 * a), mixed, bias_of(row_cut))
            window_pairs(qkv, group, (2 * a, 0), mixed, bias_of(col_cut))

    both = pl.ds(0, 2)
    back = [
        remote(mixed.at[both, 0, inner], mixed.at[both, 8, inner], back_send.at[0], back_recv.at[0], behind[0]),
        remote(mixed.at[both, inner, 0], mixed.at[both, inner, 8], back_send.at[1], back_recv.at[1], behind[1]),
        remote(mixed.at[both, 0, 0], mixed.at[both, 8, 8], back_send.at[2], back_recv.at[2], behind[2]),
    ]
    for copy in back:
        copy.start()

    @pl.loop(1, 4)
    def _(a):
        for b in range(1, 4):
            for group in range(2):
                window_pairs(qkv, group, (2 * a, 2 * b), mixed, None)

    out_weight_copy.wait()
    backward = strip_perm(True)
    for copy in back:
        copy.wait_recv()

    @pl.loop(0, 4)
    def _(part):
        sources = []
        for half in range(2):
            strip = 2 * part + half
            packed = jnp.concatenate(
                [mixed[g, strip + 1, pl.ds(1, 8)].reshape(BLOCK, GROUP) for g in range(2)], axis=1
            )
            sources.append(jnp.dot(backward, packed, preferred_element_type=jnp.float32).astype(jnp.bfloat16))
        layer_out = jnp.dot(
            jnp.concatenate(sources, axis=0), out_weight[...], preferred_element_type=jnp.float32
        )
        for half in range(2):
            strip = 2 * part + half
            tokens[strip] = (
                layer_out[BLOCK * half : BLOCK * half + BLOCK] + tokens[strip].astype(jnp.float32)
            ).astype(jnp.bfloat16)
            result_copy(strip).start()

    width = tokens.shape[2]
    slots = 8 * KSLOT
    ids = jnp.concatenate(
        [jnp.broadcast_to(parcel_ref[u : u + 1, :], (KSLOT, KSLOT)) for u in range(8)], axis=0
    )
    at = lax.broadcasted_iota(jnp.int32, (slots, KSLOT), 1) == lax.rem(
        lax.broadcasted_iota(jnp.int32, (slots, KSLOT), 0), KSLOT
    )
    ids = jnp.sum(jnp.where(at, ids.astype(jnp.float32), 0.0), axis=1, keepdims=True)
    live = ids >= 0
    ids = jnp.maximum(ids, 0.0)
    ids_high = jnp.floor(ids * (1.0 / 128.0))
    ids_low = ids - ids_high * 128.0
    place = place_ref[...]
    owner = picked(ids_high, ids_low, (place // 128).astype(jnp.float32))
    local = picked(ids_high, ids_low, (place % 128).astype(jnp.float32))
    kind = picked(owner, local, class_ref[...].astype(jnp.float32))
    power = exponent_of(kind, exponents)
    owner = jnp.where(live, owner, -1.0)
    owner_row = onto_rows(owner, slots)
    earlier = lax.broadcasted_iota(jnp.int32, (slots, slots), 1) < lax.broadcasted_iota(
        jnp.int32, (slots, slots), 0
    )
    rank = jnp.sum(jnp.where((owner == owner_row) & earlier, 1.0, 0.0), axis=1, keepdims=True)
    target = jnp.where(live, owner * 2.0 + rank, -1.0)
    target_row = onto_rows(target, slots)
    lane = lax.broadcasted_iota(jnp.int32, (KSLOT, META), 1)
    for strip in range(8):
        cut = slice(KSLOT * strip, KSLOT * strip + KSLOT)
        match = (
            lax.broadcasted_iota(jnp.int32, (KSLOT, BLOCK), 0) == jnp.concatenate([slot_ref[4 * strip + i : 4 * strip + i + 1, :] for i in range(4)], axis=1)
        ).astype(jnp.float32)
        token_power = onto_columns(jnp.sum(match * power[cut], axis=0, keepdims=True), BLOCK)
        values = jnp.maximum(tokens[strip].astype(jnp.float32), pool_floor)
        lifted = jnp.exp(token_power * jnp.log(values))
        sums[cut, 0:width] = jnp.dot(
            match.astype(jnp.bfloat16), lifted.astype(jnp.bfloat16), preferred_element_type=jnp.float32
        )
        count = jnp.sum(match, axis=1, keepdims=True)
        sums[cut, width : width + META] = jnp.where(
            lane == 0, count, jnp.where(lane == 1, local[cut], 0.0)
        )
    chooser = (
        lax.broadcasted_iota(jnp.int32, (256, slots), 0).astype(jnp.float32) == target_row
    ).astype(jnp.bfloat16)
    cuts = (slice(640, width + META), slice(0, 640))
    sends_a, recvs_a = (send_a0, send_a1), (recv_a0, recv_a1)
    sends_b, recvs_b = (send_b0, send_b1), (recv_b0, recv_b1)
    copies_a, copies_b = [], []
    for part in range(2):
        rows = jnp.dot(chooser, sums[:, cuts[part]].astype(jnp.bfloat16), preferred_element_type=jnp.float32)
        sends_a[part][...] = rows.astype(jnp.bfloat16).reshape(sends_a[part].shape)
        copies_a.append(exchange("tr", row, down, sends_a[part], recvs_a[part], send_sem_a.at[part], recv_sem_a.at[part]))
        recvs_a[part][row] = sends_a[part][row]

    def lists(at, count):
        return [adjacency[j, at * 8 + e] for e in range(8) for j in range(1, NB)]

    @pl.loop(0, 16)
    def _(there):
        least, most = jnp.int32(8), jnp.int32(-1)
        for block in lists(there, 8):
            inner_at = block - 8 * row
            mine = (inner_at >= 0) & (inner_at < 8)
            least = jnp.where(mine, jnp.minimum(least, inner_at), least)
            most = jnp.where(mine, jnp.maximum(most, inner_at), most)
        pick_out[there, 0] = jnp.minimum(least, 7)
        pick_out[there, 1] = jnp.maximum(most, 0)

    @pl.loop(0, 8)
    def _(e):
        named = lists(row, 8)
        for j in range(NB - 1):
            block = adjacency[j + 1, row * 8 + e]
            source = block // 8
            least = block
            for other in named:
                least = jnp.where(other // 8 == source, jnp.minimum(least, other), least)
            pick_in[e, j] = source * MAXB + jnp.where(block == least, 0, 1)

    for copy in quarters:
        copy.wait_send()
    for copy in wholes + relays:
        copy.wait()
    for copy in keep:
        copy.wait()
    out_at = lax.broadcasted_iota(jnp.int32, (256, 256), 0)
    in_at = lax.broadcasted_iota(jnp.int32, (256, 256), 1)
    swap = jnp.where(((out_at // 2) % 16) * 16 + (out_at // 32) * 2 + out_at % 2 == in_at, 1.0, 0.0)
    swap = swap.astype(jnp.bfloat16)
    for part in range(2):
        for copy in copies_a[part]:
            copy.wait_recv()
        arrived = recvs_a[part][...]
        rows = jnp.dot(swap, arrived.reshape(256, arrived.shape[2]), preferred_element_type=jnp.float32)
        sends_b[part][...] = rows.astype(jnp.bfloat16).reshape(sends_b[part].shape)
        copies_b.append(exchange("tc", col, across, sends_b[part], recvs_b[part], send_sem_b.at[part], recv_sem_b.at[part]))
        recvs_b[part][col] = sends_b[part][col]
    for copy in twins:
        copy.start()
    own_kind = class_ref[pl.ds(row * n_col + col, 1), :].astype(jnp.float32)
    own_power = onto_columns(exponent_of(own_kind, exponents), PARCELS_DEV)
    lane = lax.broadcasted_iota(jnp.int32, (256, PARCELS_DEV), 1).astype(jnp.float32)
    embed_copy.wait()
    placed = None
    pooled = []
    for part in range(2):
        for copy in copies_b[part]:
            copy.wait_recv()
        arrived = recvs_b[part][...]
        arrived = arrived.reshape(256, arrived.shape[2])
        if part == 0:
            info = arrived[:, 640:].astype(jnp.float32)
            count, local = info[:, 0:1], info[:, 1:2]
            placed = jnp.where((lane == local) & (count > 0), 1.0, 0.0).astype(jnp.bfloat16)
        total = lax.dot_general(placed, arrived, (((0,), (0,)), ((), ())), preferred_element_type=jnp.float32)
        if part == 0:
            counts = total[:, 640:641]
        pooled.append(jnp.exp(jnp.log(total[:, 0:640] / counts) / own_power).astype(jnp.bfloat16))
    hidden = jnp.dot(
        jnp.concatenate([pooled[1], pooled[0]], axis=1), embed[...], preferred_element_type=jnp.float32
    ).astype(jnp.bfloat16)
    normed = layer_norm(hidden.astype(jnp.float32), parcel_gain[...].reshape(1, 1024)).astype(jnp.bfloat16)

    recv_1 = (recv_1_0, recv_1_1,)
    recv_2 = (recv_2_0, recv_2_1,)
    copies_1, copies_2, copies_3 = [], [], []
    for piece in range(PIECES):
        cut = slice(PIECE * piece, PIECE * piece + PIECE)
        for part in range(8):
            send_1[piece, part] = normed[cut, P_HDIM * part : P_HDIM * part + P_HDIM]
        copies_1.append(
            exchange("tc", col, across, send_1.at[piece], recv_1[piece], send_sem_1.at[piece], recv_sem_1.at[piece])
        )
        recv_1[piece][col] = send_1[piece, col]
    for piece in range(PIECES):
        for copy in copies_1[piece]:
            copy.wait_recv()
        for peer in down:
            there = peer["tr"]
            for slot in range(MAXB):
                send_2[piece, there, slot] = recv_1[piece][pick_out[there, slot]]
        copies_2.append(
            exchange("tr", row, down, send_2.at[piece], recv_2[piece], send_sem_2.at[piece], recv_sem_2.at[piece])
        )
        recv_2[piece][row] = jnp.zeros((MAXB, PIECE, P_HDIM), jnp.bfloat16)
    for copy in twins:
        copy.wait()
    query = jnp.dot(normed, weight[0], preferred_element_type=jnp.float32).astype(jnp.bfloat16)
    keys[0:PB] = jnp.dot(normed, weight[1], preferred_element_type=jnp.float32).astype(jnp.bfloat16)
    vals[0:PB] = jnp.dot(normed, weight[2], preferred_element_type=jnp.float32).astype(jnp.bfloat16)
    for piece in range(PIECES):
        for copy in copies_2[piece]:
            copy.wait_recv()
        for there in range(8):
            for j in range(NB - 1):
                at = pick_in[there, j]
                send_3[piece, there, j] = recv_2[piece][at // MAXB, at % MAXB]
        copies_3.append(
            exchange("tc", col, across, send_3.at[piece], recv_3.at[piece], send_sem_3.at[piece], recv_sem_3.at[piece])
        )
        recv_3[piece, col] = send_3[piece, col]
    near = (NB - 1) * PIECE
    for piece in range(PIECES):
        for copy in copies_3[piece]:
            copy.wait_recv()
        source = jnp.concatenate([recv_3[piece, part].reshape(near, P_HDIM) for part in range(8)], axis=1)
        cut = slice(PB + near * piece, PB + near * piece + near)
        keys[cut] = jnp.dot(source, weight[1], preferred_element_type=jnp.float32).astype(jnp.bfloat16)
        vals[cut] = jnp.dot(source, weight[2], preferred_element_type=jnp.float32).astype(jnp.bfloat16)
    attended = []
    for head in range(8):
        cut = slice(P_HDIM * head, P_HDIM * head + P_HDIM)
        scores = lax.dot_general(
            query[:, cut], keys[:, cut], (((1,), (1,)), ((), ())), preferred_element_type=jnp.float32
        ) * P_HDIM ** (-0.5)
        weights = softmax_rows(scores).astype(jnp.bfloat16)
        attended.append(
            jnp.dot(weights, vals[:, cut], preferred_element_type=jnp.float32).astype(jnp.bfloat16)
        )
    combined = jnp.dot(
        jnp.concatenate(attended, axis=1), merge[...], preferred_element_type=jnp.float32
    )
    out_ref[...] = (combined + hidden.astype(jnp.float32)).astype(jnp.bfloat16)
    for strip in range(8):
        result_copy(strip).wait()
    for copies in [halo, back] + copies_a + copies_b + copies_1 + copies_2 + copies_3:
        for copy in copies:
            copy.wait_send()


def hand_over_kernel(tile_from, vector_from, tile_to, vector_to, tile_here, vector_here, sem):
    pairs = [(tile_from.at[i], tile_here.at[i], tile_to.at[i]) for i in range(8)]
    pairs.append((vector_from, vector_here, vector_to))
    taken = [pltpu.make_async_copy(pair[0], pair[1], sem.at[0, i]) for i, pair in enumerate(pairs)]
    given = [pltpu.make_async_copy(pair[1], pair[2], sem.at[1, i]) for i, pair in enumerate(pairs)]
    for copy in taken:
        copy.start()
    for first, second in zip(taken, given):
        first.wait()
        second.start()
    for copy in given:
        copy.wait()


def hand_over(tile, vector):
    far = pl.BlockSpec(memory_space=pltpu.HBM)
    return pl.pallas_call(
        hand_over_kernel,
        out_shape=(jax.ShapeDtypeStruct(tile.shape, tile.dtype), jax.ShapeDtypeStruct(vector.shape, vector.dtype)),
        in_specs=[far, far],
        out_specs=(far, far),
        scratch_shapes=[
            pltpu.VMEM(tile.shape, tile.dtype),
            pltpu.VMEM(vector.shape, vector.dtype),
            pltpu.SemaphoreType.DMA((2, 9)),
        ],
        compiler_params=pltpu.CompilerParams(vmem_limit_bytes=62 * 1024 * 1024),
        name="hand_over",
    )(tile, vector)


def body(
    tokens,
    norm_gain,
    window_weight,
    output_weight,
    token_slot,
    block_parcel,
    parcel_place,
    parcel_class,
    pool_exponent,
    embed_weight,
    parcel_gain,
    parcel_weight,
    merge_weight,
    adjacency,
):
    width = tokens.shape[2]
    rows_out = embed_weight.shape[1]
    far = pl.BlockSpec(memory_space=pltpu.HBM)
    near = pl.BlockSpec(memory_space=pltpu.VMEM)
    scalars = pl.BlockSpec(memory_space=pltpu.SMEM)
    bf16 = jnp.bfloat16
    dma = pltpu.SemaphoreType.DMA
    tile, vector = pl.pallas_call(
        whole_kernel,
        out_shape=(
            jax.ShapeDtypeStruct((8, BLOCK, width), bf16),
            jax.ShapeDtypeStruct((PARCELS_DEV, rows_out), bf16),
        ),
        in_specs=[far, near, far, far, far, far, near, near, near, near, scalars, far, near, scalars],
        out_specs=(far, near),
        scratch_shapes=[
            pltpu.VMEM((8, BLOCK, width), bf16),
            pltpu.VMEM((9, 9, SUB, width), bf16),
            pltpu.VMEM((6, 8, 8, SUB, GROUP), bf16),
            pltpu.VMEM((2, 9, 9, SUB, GROUP), bf16),
            pltpu.VMEM((6, width, GROUP), bf16),
            pltpu.VMEM((width, width), bf16),
            pltpu.VMEM((3, rows_out, rows_out), bf16),
            pltpu.VMEM((rows_out, rows_out), bf16),
            pltpu.VMEM((width, rows_out), bf16),
            pltpu.VMEM((8 * KSLOT, width + META), jnp.float32),
            pltpu.VMEM((16, 16, 640 + META), bf16),
            pltpu.VMEM((16, 16, 640), bf16),
            pltpu.VMEM((16, 16, 640 + META), bf16),
            pltpu.VMEM((16, 16, 640), bf16),
            pltpu.VMEM((8, 32, 640 + META), bf16),
            pltpu.VMEM((8, 32, 640), bf16),
            pltpu.VMEM((8, 32, 640 + META), bf16),
            pltpu.VMEM((8, 32, 640), bf16),
            pltpu.VMEM((PIECES, 8, PIECE, P_HDIM), bf16),
            pltpu.VMEM((PIECES, 16, MAXB, PIECE, P_HDIM), bf16),
            pltpu.VMEM((PIECES, 8, NB - 1, PIECE, P_HDIM), bf16),
            pltpu.VMEM((PIECES, 8, NB - 1, PIECE, P_HDIM), bf16),
            pltpu.VMEM((NB * PB, rows_out), bf16),
            pltpu.VMEM((NB * PB, rows_out), bf16),
            pltpu.SMEM((16, MAXB), jnp.int32),
            pltpu.SMEM((8, NB - 1), jnp.int32),
            *[pltpu.VMEM((8, PIECE, P_HDIM), bf16) for _ in range(PIECES)],
            *[pltpu.VMEM((16, MAXB, PIECE, P_HDIM), bf16) for _ in range(PIECES)],
            dma((8,)),
            dma((8,)),
            dma((8,)),
            dma((3,)),
            dma((3,)),
            dma((3,)),
            dma((3,)),
            dma((2,)),
            dma((3, 3)),
            dma((3, 3)),
            dma((2, 3, 3)),
            dma((2, 3, 3)),
            dma((2, 4)),
            dma((2, 4)),
            dma((2, 15)),
            dma((2, 15)),
            dma((2, 7)),
            dma((2, 7)),
            dma((PIECES, 7)),
            dma((PIECES, 7)),
            dma((PIECES, 15)),
            dma((PIECES, 15)),
            dma((PIECES, 7)),
            dma((PIECES, 7)),
        ],
        compiler_params=pltpu.CompilerParams(
            collective_id=1, has_side_effects=True, vmem_limit_bytes=62 * 1024 * 1024
        ),
        cost_estimate=pl.CostEstimate(flops=20 * 10**9, bytes_accessed=30 * 10**6, transcendentals=5 * 10**6),
        name="encoder_and_parcels",
    )(
        tokens.reshape(8, BLOCK, width),
        norm_gain,
        window_weight,
        output_weight,
        parcel_weight,
        merge_weight,
        token_slot,
        block_parcel.reshape(8, KSLOT),
        parcel_place.reshape(128, 128),
        parcel_class.reshape(128, 128),
        pool_exponent,
        embed_weight,
        parcel_gain,
        adjacency.T,
    )
    tile, vector = hand_over(tile, vector)
    return (tile.reshape(tokens.shape), vector)


def solution(mesh):
    return jax.shard_map(
        body,
        mesh=mesh,
        in_specs=(
            P("tr", "tc", None),
            P(),
            P(),
            P(),
            P("tr", "tc"),
            P("tr", "tc", None),
            P(),
            P(),
            P(),
            P(),
            P(),
            P(None, None, "tc"),
            P("tc", None),
            P(),
        ),
        out_specs=(P("tr", "tc", None), P(("tr", "tc"), None)),
        check_vma=False,
    )
```

```python
import jax
import jax.numpy as jnp
from jax import lax
from jax.experimental import pallas as pl
from jax.experimental.pallas import tpu as pltpu
from jax.sharding import PartitionSpec as P

HEADS = 16
HDIM = 80
BLOCK = 128
KSLOT = 24
NCLASS = 8
PARCELS_DEV = 128
P_HDIM = 128
PB = 128
NB = 4
MAXB = 2


norm_epsilon = 1e-05
pool_floor = 1e-06


def layer_norm(values, norm_gain):
    centred = values - jnp.mean(values, axis=-1, keepdims=True)
    spread = jnp.mean(centred * centred, axis=-1, keepdims=True)
    return centred * lax.rsqrt(spread + norm_epsilon) * norm_gain


def softmax_rows(scores):
    row_top = jnp.max(scores, axis=-1, keepdims=True)
    lifted = jnp.exp(scores - row_top)
    return lifted / jnp.sum(lifted, axis=-1, keepdims=True)


MESH = pl.DeviceIdType.MESH
GROUP = 640
SUB = 16
SCALE = HDIM ** (-0.5) * 1.4426950408889634


def strip_perm(flip):
    first = lax.broadcasted_iota(jnp.int32, (BLOCK, BLOCK), 0)
    second = lax.broadcasted_iota(jnp.int32, (BLOCK, BLOCK), 1)
    out_at, in_at = (second, first) if flip else (first, second)
    source = ((out_at // 4) % 4) * 32 + (out_at // 16) * 4 + out_at % 4
    return jnp.where(source == in_at, 1.0, 0.0).astype(jnp.bfloat16)


def window_pairs(qkv, group, at, mixed, bias):
    lane = lax.broadcasted_iota(jnp.int32, (1, 256), 1)
    low = lax.broadcasted_iota(jnp.int32, (1, 128), 1) < 64
    zero = jnp.zeros((), jnp.bfloat16)
    halves = (
        lax.broadcasted_iota(jnp.int32, (128, 128), 0) // 64 == lax.broadcasted_iota(jnp.int32, (128, 128), 1) // 64
    )
    halves = jnp.where(halves, 1.0, 0.0).astype(jnp.bfloat16)

    def part_of(third, pair):
        lanes = pl.ds(128 * pair, 256)
        return qkv[2 * third + group, pl.ds(at[0], 2), pl.ds(at[1], 2), :, lanes].reshape(64, 256)

    def split(values, pair):
        start = 32 * pair
        even = (lane >= start) & (lane < start + HDIM)
        odd = (lane >= start + HDIM) & (lane < start + 2 * HDIM)
        return jnp.concatenate([jnp.where(even, values, zero), jnp.where(odd, values, zero)], axis=0)

    lifted = []
    for pair in range(4):
        scores = lax.dot_general(
            part_of(0, pair), split(part_of(1, pair), pair), (((1,), (1,)), ((), ())),
            preferred_element_type=jnp.float32,
        )
        if bias is not None:
            scores = scores + bias
        top_low = jnp.max(jnp.where(low, scores, -jnp.inf), axis=-1, keepdims=True)
        top_high = jnp.max(jnp.where(low, -jnp.inf, scores), axis=-1, keepdims=True)
        lifted.append(jnp.exp2((scores - jnp.where(low, top_low, top_high)) * SCALE))
    lifted = jnp.concatenate(lifted, axis=0)
    total = jnp.dot(lifted.astype(jnp.bfloat16), halves, preferred_element_type=jnp.float32)
    weights = (lifted / total).astype(jnp.bfloat16)
    parts = [None] * 5
    for pair in range(4):
        part = jnp.dot(
            weights[64 * pair : 64 * pair + 64], split(part_of(2, pair), pair), preferred_element_type=jnp.float32
        )
        for half in range(2):
            cut = part[:, 128 * half : 128 * half + 128]
            parts[pair + half] = cut if parts[pair + half] is None else parts[pair + half] + cut
    for tile in range(5):
        mixed[group, pl.ds(at[0], 2), pl.ds(at[1], 2), :, pl.ds(128 * tile, 128)] = (
            parts[tile].astype(jnp.bfloat16).reshape(2, 2, SUB, 128)
        )


META = 128
CUTS = ((1024, 1408), (0, 384), (384, 768), (768, 1024))
PIECES = 4
PIECE = PB // PIECES


def onto_rows(column, size):
    here = lax.broadcasted_iota(jnp.int32, (size, size), 0) == lax.broadcasted_iota(jnp.int32, (size, size), 1)
    return jnp.sum(jnp.where(here, column, 0.0), axis=0, keepdims=True)


def onto_columns(row, size):
    here = lax.broadcasted_iota(jnp.int32, (size, size), 0) == lax.broadcasted_iota(jnp.int32, (size, size), 1)
    return jnp.sum(jnp.where(here, row, 0.0), axis=1, keepdims=True)


def exponent_of(kind, exponents):
    power = jnp.zeros_like(kind)
    for k in range(NCLASS):
        power = jnp.where(kind == k, exponents[k], power)
    return power


def picked(select, at, table):
    lane = lax.broadcasted_iota(jnp.int32, (select.shape[0], 128), 1).astype(jnp.float32)
    rows = jnp.dot(
        (select == lane).astype(jnp.bfloat16), table.astype(jnp.bfloat16), preferred_element_type=jnp.float32
    )
    return jnp.sum(jnp.where(at == lane, rows, 0.0), axis=1, keepdims=True)


def exchange(axis, index, peers, source, target, send_sem, recv_sem):
    copies = []
    for k, peer in enumerate(peers):
        copies.append(
            pltpu.make_async_remote_copy(
                src_ref=source.at[peer[axis]],
                dst_ref=target.at[index],
                send_sem=send_sem.at[k],
                recv_sem=recv_sem.at[k],
                device_id=peer,
                device_id_type=MESH,
            )
        )
    for copy in copies:
        copy.start()
    return copies


def whole_kernel(
    tokens_hbm, gain_ref, packed_weight_hbm, out_weight_hbm, parcel_weight_hbm, merge_hbm,
    slot_ref, parcel_ref, place_ref, class_ref, exponents, embed_hbm, parcel_gain, adjacency,
    out_hbm, out_ref,
    tokens, region, qkv, mixed, packed_weight, out_weight, weight, merge, embed, sums,
    send_a0, send_a1, send_a2, send_a3, recv_a0, recv_a1, recv_a2, recv_a3, send_b0, send_b1, send_b2, send_b3, recv_b0, recv_b1, recv_b2, recv_b3,
    send_1, send_2, send_3, recv_3, keys, vals, pick_out, pick_in, recv_1_0, recv_1_1, recv_1_2, recv_1_3, recv_2_0, recv_2_1, recv_2_2, recv_2_3,
    token_sem, weight_sem, out_sem, halo_send, halo_recv, back_send, back_recv,
    keep_sem, first_send, first_recv, second_send, second_recv, twin_send, twin_recv,
    send_sem_a, recv_sem_a, send_sem_b, recv_sem_b,
    send_sem_1, recv_sem_1, send_sem_2, recv_sem_2, send_sem_3, recv_sem_3,
):
    row = lax.axis_index("tr")
    col = lax.axis_index("tc")
    n_row = lax.axis_size("tr")
    n_col = lax.axis_size("tc")

    def token_copy(strip):
        return pltpu.make_async_copy(tokens_hbm.at[strip], tokens.at[strip], token_sem.at[strip])

    def weight_copy(chunk):
        return pltpu.make_async_copy(
            packed_weight_hbm.at[:, pl.ds(pl.multiple_of(GROUP * chunk, 128), GROUP)],
            packed_weight.at[chunk],
            weight_sem.at[chunk],
        )

    out_weight_copy = pltpu.make_async_copy(out_weight_hbm, out_weight, weight_sem.at[6])

    def result_copy(strip):
        return pltpu.make_async_copy(tokens.at[strip], out_hbm.at[strip], out_sem.at[strip])

    def remote(source, target, send, recv, peer):
        return pltpu.make_async_remote_copy(
            src_ref=source, dst_ref=target, send_sem=send, recv_sem=recv, device_id=peer, device_id_type=MESH
        )

    for strip in (7, 0, 1, 2, 3, 4, 5, 6):
        token_copy(strip).start()
    for chunk in range(6):
        weight_copy(chunk).start()
    out_weight_copy.start()
    embed_copy = pltpu.make_async_copy(embed_hbm, embed, weight_sem.at[7])
    embed_copy.start()

    def peer_at(dr, dc):
        return {"tr": lax.rem(row + dr + n_row, n_row), "tc": lax.rem(col + dc + n_col, n_col)}

    x, z = lax.rem(row, 4), row // 4
    ahead = [peer_at(1, 0), peer_at(0, 1), peer_at(1, 1)]
    behind = [peer_at(-1, 0), peer_at(0, -1), peer_at(-1, -1)]
    along_y = [peer_at(0, 2 * k) for k in range(1, 4)]
    along_x = [{"tr": z * 4 + lax.rem(x + k, 4), "tc": col} for k in range(1, 4)]
    along_z = [{"tr": lax.rem(z + k, 4) * 4 + x, "tc": col} for k in range(1, 4)]
    down = [peer_at(k, 0) for k in range(1, n_row)]
    across = [peer_at(0, k) for k in range(1, n_col)]
    peers = down + across + [ahead[2], behind[2]]
    barrier = pltpu.get_barrier_semaphore()
    for peer in peers:
        pl.semaphore_signal(barrier, inc=1, device_id=peer, device_id_type=MESH)

    forward = strip_perm(False)

    def norm_strip(strip):
        token_copy(strip).wait()
        values = jnp.dot(forward, tokens[strip], preferred_element_type=jnp.float32)
        normed = layer_norm(values, gain_ref[...].reshape(1, 1280)).astype(jnp.bfloat16)
        region[strip + 1, pl.ds(1, 8)] = normed.reshape(8, SUB, 1280)

    norm_strip(7)
    pl.semaphore_wait(barrier, len(peers))
    inner = pl.ds(1, 7)
    halo = [
        remote(region.at[8, inner], region.at[0, inner], halo_send.at[0], halo_recv.at[0], ahead[0]),
        remote(region.at[inner, 8], region.at[inner, 0], halo_send.at[1], halo_recv.at[1], ahead[1]),
        remote(region.at[8, 8], region.at[0, 0], halo_send.at[2], halo_recv.at[2], ahead[2]),
    ]
    halo[0].start()
    halo[2].start()

    @pl.loop(0, 7)
    def _(strip):
        norm_strip(strip)

    halo[1].start()
    x_rows = pl.ds(pl.multiple_of(256 * x, 256), 256)

    def lanes_of(head):
        return pl.ds(pl.multiple_of(P_HDIM * head, P_HDIM), P_HDIM)

    def merge_rows(head):
        return pl.ds(pl.multiple_of(P_HDIM * head + 32 * z, 32), 32)

    own = lanes_of(col)
    keep = [
        pltpu.make_async_copy(parcel_weight_hbm, weight.at[:, :, own], keep_sem.at[0]),
        pltpu.make_async_copy(merge_hbm, merge.at[own], keep_sem.at[1]),
    ]
    quarters, wholes, relays, twins = [], [], [], []
    twin = {"tr": row, "tc": col + 1 - 2 * lax.rem(col, 2)}
    for k, peer in enumerate(along_y):
        quarters.append(
            remote(
                parcel_weight_hbm.at[0, x_rows], weight.at[0, x_rows, own],
                first_send.at[0, k], first_recv.at[0, k], peer,
            )
        )
        quarters.append(
            remote(
                merge_hbm.at[pl.ds(pl.multiple_of(32 * z, 32), 32)], merge.at[merge_rows(col)],
                first_send.at[1, k], first_recv.at[1, k], peer,
            )
        )
        wholes.append(
            remote(
                parcel_weight_hbm.at[pl.ds(1, 2)], weight.at[pl.ds(1, 2), :, own],
                first_send.at[2, k], first_recv.at[2, k], peer,
            )
        )
        there = lax.rem(col + 2 * (k + 1), n_col)
        for j in range(3):
            q_part = weight.at[0, x_rows, lanes_of(there)]
            relays.append(remote(q_part, q_part, second_send.at[0, k, j], second_recv.at[0, k, j], along_x[j]))
            merge_part = merge.at[merge_rows(there)]
            relays.append(
                remote(merge_part, merge_part, second_send.at[1, k, j], second_recv.at[1, k, j], along_z[j])
            )
    for k in range(4):
        there = lanes_of(lax.rem(col + 2 * k, n_col))
        for j, part in enumerate((weight.at[:, :, there], merge.at[there])):
            twins.append(remote(part, part, twin_send.at[j, k], twin_recv.at[j, k], twin))
    for copy in quarters + wholes + keep:
        copy.start()

    @pl.loop(0, 6)
    def _(chunk):
        weight_copy(chunk).wait()
        source = region[inner, inner].reshape(784, 1280)
        packed = jnp.dot(source, packed_weight[chunk], preferred_element_type=jnp.float32)
        qkv[chunk, inner, inner] = packed.astype(jnp.bfloat16).reshape(7, 7, SUB, GROUP)

    for copy in quarters:
        copy.wait_recv()
    for copy in relays:
        copy.start()
    for copy in halo:
        copy.wait_recv()

    @pl.loop(0, 6)
    def _(chunk):
        source = jnp.concatenate(
            [region[0, pl.ds(0, 8)].reshape(128, 1280), region[inner, 0].reshape(112, 1280)], axis=0
        )
        packed = jnp.dot(source, packed_weight[chunk], preferred_element_type=jnp.float32).astype(jnp.bfloat16)
        qkv[chunk, 0] = packed[0:128].reshape(8, SUB, GROUP)
        qkv[chunk, inner, 0] = packed[128:240].reshape(7, SUB, GROUP)

    key_at = lax.broadcasted_iota(jnp.int32, (64, 128), 1) % 64
    query_at = lax.broadcasted_iota(jnp.int32, (64, 128), 0)
    row_cut = (key_at // 32 != query_at // 32) & (row == 0)
    col_cut = ((key_at // 16) % 2 != (query_at // 16) % 2) & (col == 0)

    def bias_of(cut):
        return jnp.where(cut, -1e30, 0.0)

    for group in range(2):
        window_pairs(qkv, group, (0, 0), mixed, bias_of(row_cut | col_cut))

    @pl.loop(1, 4)
    def _(a):
        for group in range(2):
            window_pairs(qkv, group, (0, 2 * a), mixed, bias_of(row_cut))
            window_pairs(qkv, group, (2 * a, 0), mixed, bias_of(col_cut))

    both = pl.ds(0, 2)
    back = [
        remote(mixed.at[both, 0, inner], mixed.at[both, 8, inner], back_send.at[0], back_recv.at[0], behind[0]),
        remote(mixed.at[both, inner, 0], mixed.at[both, inner, 8], back_send.at[1], back_recv.at[1], behind[1]),
        remote(mixed.at[both, 0, 0], mixed.at[both, 8, 8], back_send.at[2], back_recv.at[2], behind[2]),
    ]
    for copy in back:
        copy.start()

    @pl.loop(1, 4)
    def _(a):
        for b in range(1, 4):
            for group in range(2):
                window_pairs(qkv, group, (2 * a, 2 * b), mixed, None)

    out_weight_copy.wait()
    backward = strip_perm(True)
    for copy in back:
        copy.wait_recv()

    @pl.loop(0, 4)
    def _(part):
        sources = []
        for half in range(2):
            strip = 2 * part + half
            packed = jnp.concatenate(
                [mixed[g, strip + 1, pl.ds(1, 8)].reshape(BLOCK, GROUP) for g in range(2)], axis=1
            )
            sources.append(jnp.dot(backward, packed, preferred_element_type=jnp.float32).astype(jnp.bfloat16))
        layer_out = jnp.dot(
            jnp.concatenate(sources, axis=0), out_weight[...], preferred_element_type=jnp.float32
        )
        for half in range(2):
            strip = 2 * part + half
            tokens[strip] = (
                layer_out[BLOCK * half : BLOCK * half + BLOCK] + tokens[strip].astype(jnp.float32)
            ).astype(jnp.bfloat16)
            result_copy(strip).start()

    width = tokens.shape[2]
    slots = 8 * KSLOT
    ids = jnp.concatenate(
        [jnp.broadcast_to(parcel_ref[u : u + 1, :], (KSLOT, KSLOT)) for u in range(8)], axis=0
    )
    at = lax.broadcasted_iota(jnp.int32, (slots, KSLOT), 1) == lax.rem(
        lax.broadcasted_iota(jnp.int32, (slots, KSLOT), 0), KSLOT
    )
    ids = jnp.sum(jnp.where(at, ids.astype(jnp.float32), 0.0), axis=1, keepdims=True)
    live = ids >= 0
    ids = jnp.maximum(ids, 0.0)
    ids_high = jnp.floor(ids * (1.0 / 128.0))
    ids_low = ids - ids_high * 128.0
    place = place_ref[...]
    owner = picked(ids_high, ids_low, (place // 128).astype(jnp.float32))
    local = picked(ids_high, ids_low, (place % 128).astype(jnp.float32))
    kind = picked(owner, local, class_ref[...].astype(jnp.float32))
    power = exponent_of(kind, exponents)
    owner = jnp.where(live, owner, -1.0)
    owner_row = onto_rows(owner, slots)
    earlier = lax.broadcasted_iota(jnp.int32, (slots, slots), 1) < lax.broadcasted_iota(
        jnp.int32, (slots, slots), 0
    )
    rank = jnp.sum(jnp.where((owner == owner_row) & earlier, 1.0, 0.0), axis=1, keepdims=True)
    target = jnp.where(live, owner * 2.0 + rank, -1.0)
    target_row = onto_rows(target, slots)
    lane = lax.broadcasted_iota(jnp.int32, (KSLOT, META), 1)
    for strip in range(8):
        cut = slice(KSLOT * strip, KSLOT * strip + KSLOT)
        match = (
            lax.broadcasted_iota(jnp.int32, (KSLOT, BLOCK), 0) == jnp.concatenate([slot_ref[4 * strip + i : 4 * strip + i + 1, :] for i in range(4)], axis=1)
        ).astype(jnp.float32)
        token_power = onto_columns(jnp.sum(match * power[cut], axis=0, keepdims=True), BLOCK)
        values = jnp.maximum(tokens[strip].astype(jnp.float32), pool_floor)
        lifted = jnp.exp(token_power * jnp.log(values))
        sums[cut, 0:width] = jnp.dot(
            match.astype(jnp.bfloat16), lifted.astype(jnp.bfloat16), preferred_element_type=jnp.float32
        )
        count = jnp.sum(match, axis=1, keepdims=True)
        sums[cut, width : width + META] = jnp.where(
            lane == 0, count, jnp.where(lane == 1, local[cut], 0.0)
        )
    chooser = (
        lax.broadcasted_iota(jnp.int32, (256, slots), 0).astype(jnp.float32) == target_row
    ).astype(jnp.bfloat16)
    parts = range(len(CUTS))
    sends_a, recvs_a = (send_a0, send_a1, send_a2, send_a3,), (recv_a0, recv_a1, recv_a2, recv_a3,)
    sends_b, recvs_b = (send_b0, send_b1, send_b2, send_b3,), (recv_b0, recv_b1, recv_b2, recv_b3,)
    copies_a, copies_b = [], []
    for part in parts:
        rows = jnp.dot(chooser, sums[:, CUTS[part][0] : CUTS[part][1]].astype(jnp.bfloat16), preferred_element_type=jnp.float32)
        sends_a[part][...] = rows.astype(jnp.bfloat16).reshape(sends_a[part].shape)
        copies_a.append(exchange("tr", row, down, sends_a[part], recvs_a[part], send_sem_a.at[part], recv_sem_a.at[part]))
        recvs_a[part][row] = sends_a[part][row]

    def lists(at, count):
        return [adjacency[j, at * 8 + e] for e in range(8) for j in range(1, NB)]

    @pl.loop(0, 16)
    def _(there):
        least, most = jnp.int32(8), jnp.int32(-1)
        for block in lists(there, 8):
            inner_at = block - 8 * row
            mine = (inner_at >= 0) & (inner_at < 8)
            least = jnp.where(mine, jnp.minimum(least, inner_at), least)
            most = jnp.where(mine, jnp.maximum(most, inner_at), most)
        pick_out[there, 0] = jnp.minimum(least, 7)
        pick_out[there, 1] = jnp.maximum(most, 0)

    @pl.loop(0, 8)
    def _(e):
        named = lists(row, 8)
        for j in range(NB - 1):
            block = adjacency[j + 1, row * 8 + e]
            source = block // 8
            least = block
            for other in named:
                least = jnp.where(other // 8 == source, jnp.minimum(least, other), least)
            pick_in[e, j] = source * MAXB + jnp.where(block == least, 0, 1)

    for copy in quarters:
        copy.wait_send()
    for copy in wholes + relays:
        copy.wait()
    for copy in keep:
        copy.wait()
    for copy in twins:
        copy.start()
    out_at = lax.broadcasted_iota(jnp.int32, (256, 256), 0)
    in_at = lax.broadcasted_iota(jnp.int32, (256, 256), 1)
    swap = jnp.where(((out_at // 2) % 16) * 16 + (out_at // 32) * 2 + out_at % 2 == in_at, 1.0, 0.0)
    swap = swap.astype(jnp.bfloat16)
    for part in parts:
        for copy in copies_a[part]:
            copy.wait_recv()
        arrived = recvs_a[part][...]
        rows = jnp.dot(swap, arrived.reshape(256, arrived.shape[2]), preferred_element_type=jnp.float32)
        sends_b[part][...] = rows.astype(jnp.bfloat16).reshape(sends_b[part].shape)
        copies_b.append(exchange("tc", col, across, sends_b[part], recvs_b[part], send_sem_b.at[part], recv_sem_b.at[part]))
        recvs_b[part][col] = sends_b[part][col]
    own_kind = class_ref[pl.ds(row * n_col + col, 1), :].astype(jnp.float32)
    own_power = onto_columns(exponent_of(own_kind, exponents), PARCELS_DEV)
    lane = lax.broadcasted_iota(jnp.int32, (256, PARCELS_DEV), 1).astype(jnp.float32)
    embed_copy.wait()
    placed = None
    pooled = []
    for part in parts:
        for copy in copies_b[part]:
            copy.wait_recv()
        arrived = recvs_b[part][...]
        arrived = arrived.reshape(256, arrived.shape[2])
        if part == 0:
            split = arrived.shape[1] - META
            info = arrived[:, split:].astype(jnp.float32)
            count, local = info[:, 0:1], info[:, 1:2]
            placed = jnp.where((lane == local) & (count > 0), 1.0, 0.0).astype(jnp.bfloat16)
        total = lax.dot_general(placed, arrived, (((0,), (0,)), ((), ())), preferred_element_type=jnp.float32)
        if part == 0:
            counts = total[:, split : split + 1]
            total = total[:, 0:split]
        pooled.append(jnp.exp(jnp.log(total / counts) / own_power).astype(jnp.bfloat16))
    hidden = jnp.dot(
        jnp.concatenate(pooled[1:] + pooled[:1], axis=1), embed[...], preferred_element_type=jnp.float32
    ).astype(jnp.bfloat16)
    normed = layer_norm(hidden.astype(jnp.float32), parcel_gain[...].reshape(1, 1024)).astype(jnp.bfloat16)

    recv_1 = (recv_1_0, recv_1_1, recv_1_2, recv_1_3,)
    recv_2 = (recv_2_0, recv_2_1, recv_2_2, recv_2_3,)
    copies_1, copies_2, copies_3 = [], [], []
    for piece in range(PIECES):
        cut = slice(PIECE * piece, PIECE * piece + PIECE)
        for part in range(8):
            send_1[piece, part] = normed[cut, P_HDIM * part : P_HDIM * part + P_HDIM]
        copies_1.append(
            exchange("tc", col, across, send_1.at[piece], recv_1[piece], send_sem_1.at[piece], recv_sem_1.at[piece])
        )
        recv_1[piece][col] = send_1[piece, col]
    for piece in range(PIECES):
        for copy in copies_1[piece]:
            copy.wait_recv()
        for peer in down:
            there = peer["tr"]
            for slot in range(MAXB):
                send_2[piece, there, slot] = recv_1[piece][pick_out[there, slot]]
        copies_2.append(
            exchange("tr", row, down, send_2.at[piece], recv_2[piece], send_sem_2.at[piece], recv_sem_2.at[piece])
        )
        recv_2[piece][row] = jnp.zeros((MAXB, PIECE, P_HDIM), jnp.bfloat16)
    for copy in twins:
        copy.wait()
    query = jnp.dot(normed, weight[0], preferred_element_type=jnp.float32).astype(jnp.bfloat16)
    keys[0:PB] = jnp.dot(normed, weight[1], preferred_element_type=jnp.float32).astype(jnp.bfloat16)
    vals[0:PB] = jnp.dot(normed, weight[2], preferred_element_type=jnp.float32).astype(jnp.bfloat16)
    for piece in range(PIECES):
        for copy in copies_2[piece]:
            copy.wait_recv()
        for there in range(8):
            for j in range(NB - 1):
                at = pick_in[there, j]
                send_3[piece, there, j] = recv_2[piece][at // MAXB, at % MAXB]
        copies_3.append(
            exchange("tc", col, across, send_3.at[piece], recv_3.at[piece], send_sem_3.at[piece], recv_sem_3.at[piece])
        )
        recv_3[piece, col] = send_3[piece, col]
    near = (NB - 1) * PIECE
    for piece in range(PIECES):
        for copy in copies_3[piece]:
            copy.wait_recv()
        source = jnp.concatenate([recv_3[piece, part].reshape(near, P_HDIM) for part in range(8)], axis=1)
        cut = slice(PB + near * piece, PB + near * piece + near)
        keys[cut] = jnp.dot(source, weight[1], preferred_element_type=jnp.float32).astype(jnp.bfloat16)
        vals[cut] = jnp.dot(source, weight[2], preferred_element_type=jnp.float32).astype(jnp.bfloat16)
    attended = []
    for head in range(8):
        cut = slice(P_HDIM * head, P_HDIM * head + P_HDIM)
        scores = lax.dot_general(
            query[:, cut], keys[:, cut], (((1,), (1,)), ((), ())), preferred_element_type=jnp.float32
        ) * P_HDIM ** (-0.5)
        weights = softmax_rows(scores).astype(jnp.bfloat16)
        attended.append(
            jnp.dot(weights, vals[:, cut], preferred_element_type=jnp.float32).astype(jnp.bfloat16)
        )
    combined = jnp.dot(
        jnp.concatenate(attended, axis=1), merge[...], preferred_element_type=jnp.float32
    )
    out_ref[...] = (combined + hidden.astype(jnp.float32)).astype(jnp.bfloat16)
    for strip in range(8):
        result_copy(strip).wait()
    for copies in [halo, back] + copies_a + copies_b + copies_1 + copies_2 + copies_3:
        for copy in copies:
            copy.wait_send()


def hand_over_kernel(tile_from, vector_from, tile_to, vector_to, tile_here, vector_here, sem):
    pairs = [(tile_from.at[i], tile_here.at[i], tile_to.at[i]) for i in range(8)]
    pairs.append((vector_from, vector_here, vector_to))
    taken = [pltpu.make_async_copy(pair[0], pair[1], sem.at[0, i]) for i, pair in enumerate(pairs)]
    given = [pltpu.make_async_copy(pair[1], pair[2], sem.at[1, i]) for i, pair in enumerate(pairs)]
    for copy in taken:
        copy.start()
    for first, second in zip(taken, given):
        first.wait()
        second.start()
    for copy in given:
        copy.wait()


def hand_over(tile, vector):
    far = pl.BlockSpec(memory_space=pltpu.HBM)
    return pl.pallas_call(
        hand_over_kernel,
        out_shape=(jax.ShapeDtypeStruct(tile.shape, tile.dtype), jax.ShapeDtypeStruct(vector.shape, vector.dtype)),
        in_specs=[far, far],
        out_specs=(far, far),
        scratch_shapes=[
            pltpu.VMEM(tile.shape, tile.dtype),
            pltpu.VMEM(vector.shape, vector.dtype),
            pltpu.SemaphoreType.DMA((2, 9)),
        ],
        compiler_params=pltpu.CompilerParams(vmem_limit_bytes=62 * 1024 * 1024),
        name="hand_over",
    )(tile, vector)


def body(
    tokens,
    norm_gain,
    window_weight,
    output_weight,
    token_slot,
    block_parcel,
    parcel_place,
    parcel_class,
    pool_exponent,
    embed_weight,
    parcel_gain,
    parcel_weight,
    merge_weight,
    adjacency,
):
    width = tokens.shape[2]
    rows_out = embed_weight.shape[1]
    far = pl.BlockSpec(memory_space=pltpu.HBM)
    near = pl.BlockSpec(memory_space=pltpu.VMEM)
    scalars = pl.BlockSpec(memory_space=pltpu.SMEM)
    bf16 = jnp.bfloat16
    dma = pltpu.SemaphoreType.DMA
    tile, vector = pl.pallas_call(
        whole_kernel,
        out_shape=(
            jax.ShapeDtypeStruct((8, BLOCK, width), bf16),
            jax.ShapeDtypeStruct((PARCELS_DEV, rows_out), bf16),
        ),
        in_specs=[far, near, far, far, far, far, near, near, near, near, scalars, far, near, scalars],
        out_specs=(far, near),
        scratch_shapes=[
            pltpu.VMEM((8, BLOCK, width), bf16),
            pltpu.VMEM((9, 9, SUB, width), bf16),
            pltpu.VMEM((6, 8, 8, SUB, GROUP), bf16),
            pltpu.VMEM((2, 9, 9, SUB, GROUP), bf16),
            pltpu.VMEM((6, width, GROUP), bf16),
            pltpu.VMEM((width, width), bf16),
            pltpu.VMEM((3, rows_out, rows_out), bf16),
            pltpu.VMEM((rows_out, rows_out), bf16),
            pltpu.VMEM((width, rows_out), bf16),
            pltpu.VMEM((8 * KSLOT, width + META), jnp.float32),
            *[pltpu.VMEM((16, 16, high - low), bf16) for _ in range(2) for low, high in CUTS],
            *[pltpu.VMEM((8, 32, high - low), bf16) for _ in range(2) for low, high in CUTS],
            pltpu.VMEM((PIECES, 8, PIECE, P_HDIM), bf16),
            pltpu.VMEM((PIECES, 16, MAXB, PIECE, P_HDIM), bf16),
            pltpu.VMEM((PIECES, 8, NB - 1, PIECE, P_HDIM), bf16),
            pltpu.VMEM((PIECES, 8, NB - 1, PIECE, P_HDIM), bf16),
            pltpu.VMEM((NB * PB, rows_out), bf16),
            pltpu.VMEM((NB * PB, rows_out), bf16),
            pltpu.SMEM((16, MAXB), jnp.int32),
            pltpu.SMEM((8, NB - 1), jnp.int32),
            *[pltpu.VMEM((8, PIECE, P_HDIM), bf16) for _ in range(PIECES)],
            *[pltpu.VMEM((16, MAXB, PIECE, P_HDIM), bf16) for _ in range(PIECES)],
            dma((8,)),
            dma((8,)),
            dma((8,)),
            dma((3,)),
            dma((3,)),
            dma((3,)),
            dma((3,)),
            dma((2,)),
            dma((3, 3)),
            dma((3, 3)),
            dma((2, 3, 3)),
            dma((2, 3, 3)),
            dma((2, 4)),
            dma((2, 4)),
            dma((len(CUTS), 15)),
            dma((len(CUTS), 15)),
            dma((len(CUTS), 7)),
            dma((len(CUTS), 7)),
            dma((PIECES, 7)),
            dma((PIECES, 7)),
            dma((PIECES, 15)),
            dma((PIECES, 15)),
            dma((PIECES, 7)),
            dma((PIECES, 7)),
        ],
        compiler_params=pltpu.CompilerParams(
            collective_id=1, has_side_effects=True, vmem_limit_bytes=62 * 1024 * 1024
        ),
        cost_estimate=pl.CostEstimate(flops=20 * 10**9, bytes_accessed=30 * 10**6, transcendentals=5 * 10**6),
        name="encoder_and_parcels",
    )(
        tokens.reshape(8, BLOCK, width),
        norm_gain,
        window_weight,
        output_weight,
        parcel_weight,
        merge_weight,
        token_slot,
        block_parcel.reshape(8, KSLOT),
        parcel_place.reshape(128, 128),
        parcel_class.reshape(128, 128),
        pool_exponent,
        embed_weight,
        parcel_gain,
        adjacency.T,
    )
    tile, vector = hand_over(tile, vector)
    return (tile.reshape(tokens.shape), vector)


def solution(mesh):
    return jax.shard_map(
        body,
        mesh=mesh,
        in_specs=(
            P("tr", "tc", None),
            P(),
            P(),
            P(),
            P("tr", "tc"),
            P("tr", "tc", None),
            P(),
            P(),
            P(),
            P(),
            P(),
            P(None, None, "tc"),
            P("tc", None),
            P(),
        ),
        out_specs=(P("tr", "tc", None), P(("tr", "tc"), None)),
        check_vma=False,
    )
```

```python
import jax
import jax.numpy as jnp
from jax import lax
from jax.experimental import pallas as pl
from jax.experimental.pallas import tpu as pltpu
from jax.sharding import PartitionSpec as P

HEADS = 16
HDIM = 80
BLOCK = 128
KSLOT = 24
NCLASS = 8
PARCELS_DEV = 128
P_HDIM = 128
PB = 128
NB = 4
MAXB = 2


norm_epsilon = 1e-05
pool_floor = 1e-06


def layer_norm(values, norm_gain):
    centred = values - jnp.mean(values, axis=-1, keepdims=True)
    spread = jnp.mean(centred * centred, axis=-1, keepdims=True)
    return centred * lax.rsqrt(spread + norm_epsilon) * norm_gain


def softmax_rows(scores):
    row_top = jnp.max(scores, axis=-1, keepdims=True)
    lifted = jnp.exp(scores - row_top)
    return lifted / jnp.sum(lifted, axis=-1, keepdims=True)


MESH = pl.DeviceIdType.MESH
GROUP = 640
SUB = 16
SCALE = HDIM ** (-0.5) * 1.4426950408889634


def strip_perm(flip):
    first = lax.broadcasted_iota(jnp.int32, (BLOCK, BLOCK), 0)
    second = lax.broadcasted_iota(jnp.int32, (BLOCK, BLOCK), 1)
    out_at, in_at = (second, first) if flip else (first, second)
    source = ((out_at // 4) % 4) * 32 + (out_at // 16) * 4 + out_at % 4
    return jnp.where(source == in_at, 1.0, 0.0).astype(jnp.bfloat16)


def window_pairs(qkv, group, at, mixed, bias):
    lane = lax.broadcasted_iota(jnp.int32, (1, 256), 1)
    low = lax.broadcasted_iota(jnp.int32, (1, 128), 1) < 64
    zero = jnp.zeros((), jnp.bfloat16)
    halves = (
        lax.broadcasted_iota(jnp.int32, (128, 128), 0) // 64 == lax.broadcasted_iota(jnp.int32, (128, 128), 1) // 64
    )
    halves = jnp.where(halves, 1.0, 0.0).astype(jnp.bfloat16)

    def part_of(third, pair):
        lanes = pl.ds(128 * pair, 256)
        return qkv[2 * third + group, pl.ds(at[0], 2), pl.ds(at[1], 2), :, lanes].reshape(64, 256)

    def split(values, pair):
        start = 32 * pair
        even = (lane >= start) & (lane < start + HDIM)
        odd = (lane >= start + HDIM) & (lane < start + 2 * HDIM)
        return jnp.concatenate([jnp.where(even, values, zero), jnp.where(odd, values, zero)], axis=0)

    lifted = []
    for pair in range(4):
        scores = lax.dot_general(
            part_of(0, pair), split(part_of(1, pair), pair), (((1,), (1,)), ((), ())),
            preferred_element_type=jnp.float32,
        )
        if bias is not None:
            scores = scores + bias
        top_low = jnp.max(jnp.where(low, scores, -jnp.inf), axis=-1, keepdims=True)
        top_high = jnp.max(jnp.where(low, -jnp.inf, scores), axis=-1, keepdims=True)
        lifted.append(jnp.exp2((scores - jnp.where(low, top_low, top_high)) * SCALE))
    lifted = jnp.concatenate(lifted, axis=0)
    total = jnp.dot(lifted.astype(jnp.bfloat16), halves, preferred_element_type=jnp.float32)
    weights = (lifted / total).astype(jnp.bfloat16)
    parts = [None] * 5
    for pair in range(4):
        part = jnp.dot(
            weights[64 * pair : 64 * pair + 64], split(part_of(2, pair), pair), preferred_element_type=jnp.float32
        )
        for half in range(2):
            cut = part[:, 128 * half : 128 * half + 128]
            parts[pair + half] = cut if parts[pair + half] is None else parts[pair + half] + cut
    for tile in range(5):
        mixed[group, pl.ds(at[0], 2), pl.ds(at[1], 2), :, pl.ds(128 * tile, 128)] = (
            parts[tile].astype(jnp.bfloat16).reshape(2, 2, SUB, 128)
        )


META = 128
CUTS = ((1024, 1408), (0, 384), (384, 768), (768, 1024))
PIECES = 4
PIECE = PB // PIECES


def onto_rows(column, size):
    here = lax.broadcasted_iota(jnp.int32, (size, size), 0) == lax.broadcasted_iota(jnp.int32, (size, size), 1)
    return jnp.sum(jnp.where(here, column, 0.0), axis=0, keepdims=True)


def onto_columns(row, size):
    here = lax.broadcasted_iota(jnp.int32, (size, size), 0) == lax.broadcasted_iota(jnp.int32, (size, size), 1)
    return jnp.sum(jnp.where(here, row, 0.0), axis=1, keepdims=True)


def exponent_of(kind, exponents):
    power = jnp.zeros_like(kind)
    for k in range(NCLASS):
        power = jnp.where(kind == k, exponents[k], power)
    return power


def picked(select, at, table):
    lane = lax.broadcasted_iota(jnp.int32, (select.shape[0], 128), 1).astype(jnp.float32)
    rows = jnp.dot(
        (select == lane).astype(jnp.bfloat16), table.astype(jnp.bfloat16), preferred_element_type=jnp.float32
    )
    return jnp.sum(jnp.where(at == lane, rows, 0.0), axis=1, keepdims=True)


def exchange(axis, index, peers, source, target, send_sem, recv_sem):
    copies = []
    for k, peer in enumerate(peers):
        copies.append(
            pltpu.make_async_remote_copy(
                src_ref=source.at[peer[axis]],
                dst_ref=target.at[index],
                send_sem=send_sem.at[k],
                recv_sem=recv_sem.at[k],
                device_id=peer,
                device_id_type=MESH,
            )
        )
    for copy in copies:
        copy.start()
    return copies


def whole_kernel(
    tokens_hbm, gain_ref, packed_weight_hbm, out_weight_hbm, parcel_weight_hbm, merge_hbm,
    slot_ref, parcel_ref, place_ref, class_ref, exponents, embed_hbm, parcel_gain, adjacency,
    out_hbm, out_ref,
    tokens, region, qkv, mixed, packed_weight, out_weight, weight, merge, embed, sums,
    send_a0, send_a1, send_a2, send_a3, recv_a0, recv_a1, recv_a2, recv_a3, send_b0, send_b1, send_b2, send_b3, recv_b0, recv_b1, recv_b2, recv_b3,
    send_1, send_2, send_3, recv_3, keys, vals, pick_out, pick_in, recv_1_0, recv_1_1, recv_1_2, recv_1_3, recv_2_0, recv_2_1, recv_2_2, recv_2_3,
    token_sem, weight_sem, out_sem, halo_send, halo_recv, back_send, back_recv,
    keep_sem, first_send, first_recv, second_send, second_recv, twin_send, twin_recv,
    send_sem_a, recv_sem_a, send_sem_b, recv_sem_b,
    send_sem_1, recv_sem_1, send_sem_2, recv_sem_2, send_sem_3, recv_sem_3,
):
    row = lax.axis_index("tr")
    col = lax.axis_index("tc")
    n_row = lax.axis_size("tr")
    n_col = lax.axis_size("tc")

    def token_copy(strip):
        return pltpu.make_async_copy(tokens_hbm.at[strip], tokens.at[strip], token_sem.at[strip])

    def weight_copy(chunk):
        return pltpu.make_async_copy(
            packed_weight_hbm.at[:, pl.ds(pl.multiple_of(GROUP * chunk, 128), GROUP)],
            packed_weight.at[chunk],
            weight_sem.at[chunk],
        )

    out_weight_copy = pltpu.make_async_copy(out_weight_hbm, out_weight, weight_sem.at[6])

    def result_copy(strip):
        return pltpu.make_async_copy(tokens.at[strip], out_hbm.at[strip], out_sem.at[strip])

    def remote(source, target, send, recv, peer):
        return pltpu.make_async_remote_copy(
            src_ref=source, dst_ref=target, send_sem=send, recv_sem=recv, device_id=peer, device_id_type=MESH
        )

    for strip in (7, 0, 1, 2, 3, 4, 5, 6):
        token_copy(strip).start()
    for chunk in range(6):
        weight_copy(chunk).start()
    out_weight_copy.start()
    embed_copy = pltpu.make_async_copy(embed_hbm, embed, weight_sem.at[7])
    embed_copy.start()

    def peer_at(dr, dc):
        return {"tr": lax.rem(row + dr + n_row, n_row), "tc": lax.rem(col + dc + n_col, n_col)}

    x, z = lax.rem(row, 4), row // 4
    ahead = [peer_at(1, 0), peer_at(0, 1), peer_at(1, 1)]
    behind = [peer_at(-1, 0), peer_at(0, -1), peer_at(-1, -1)]
    along_y = [peer_at(0, 2 * k) for k in range(1, 4)]
    along_x = [{"tr": z * 4 + lax.rem(x + k, 4), "tc": col} for k in range(1, 4)]
    along_z = [{"tr": lax.rem(z + k, 4) * 4 + x, "tc": col} for k in range(1, 4)]
    down = [peer_at(k, 0) for k in range(1, n_row)]
    across = [peer_at(0, k) for k in range(1, n_col)]
    peers = down + across + [ahead[2], behind[2]]
    barrier = pltpu.get_barrier_semaphore()
    for peer in peers:
        pl.semaphore_signal(barrier, inc=1, device_id=peer, device_id_type=MESH)

    forward = strip_perm(False)

    def norm_strip(strip):
        token_copy(strip).wait()
        values = jnp.dot(forward, tokens[strip], preferred_element_type=jnp.float32)
        normed = layer_norm(values, gain_ref[...].reshape(1, 1280)).astype(jnp.bfloat16)
        region[strip + 1, pl.ds(1, 8)] = normed.reshape(8, SUB, 1280)

    norm_strip(7)
    pl.semaphore_wait(barrier, len(peers))
    inner = pl.ds(1, 7)
    halo = [
        remote(region.at[8, inner], region.at[0, inner], halo_send.at[0], halo_recv.at[0], ahead[0]),
        remote(region.at[inner, 8], region.at[inner, 0], halo_send.at[1], halo_recv.at[1], ahead[1]),
        remote(region.at[8, 8], region.at[0, 0], halo_send.at[2], halo_recv.at[2], ahead[2]),
    ]
    halo[0].start()
    halo[2].start()

    @pl.loop(0, 7)
    def _(strip):
        norm_strip(strip)

    halo[1].start()
    x_rows = pl.ds(pl.multiple_of(256 * x, 256), 256)

    def lanes_of(head):
        return pl.ds(pl.multiple_of(P_HDIM * head, P_HDIM), P_HDIM)

    def merge_rows(head):
        return pl.ds(pl.multiple_of(P_HDIM * head + 32 * z, 32), 32)

    own = lanes_of(col)
    keep = [
        pltpu.make_async_copy(parcel_weight_hbm, weight.at[:, :, own], keep_sem.at[0]),
        pltpu.make_async_copy(merge_hbm, merge.at[own], keep_sem.at[1]),
    ]
    quarters, wholes, relays, twins = [], [], [], []
    twin = {"tr": row, "tc": col + 1 - 2 * lax.rem(col, 2)}
    for k, peer in enumerate(along_y):
        quarters.append(
            remote(
                parcel_weight_hbm.at[0, x_rows], weight.at[0, x_rows, own],
                first_send.at[0, k], first_recv.at[0, k], peer,
            )
        )
        quarters.append(
            remote(
                merge_hbm.at[pl.ds(pl.multiple_of(32 * z, 32), 32)], merge.at[merge_rows(col)],
                first_send.at[1, k], first_recv.at[1, k], peer,
            )
        )
        wholes.append(
            remote(
                parcel_weight_hbm.at[pl.ds(1, 2)], weight.at[pl.ds(1, 2), :, own],
                first_send.at[2, k], first_recv.at[2, k], peer,
            )
        )
        there = lax.rem(col + 2 * (k + 1), n_col)
        for j in range(3):
            q_part = weight.at[0, x_rows, lanes_of(there)]
            relays.append(remote(q_part, q_part, second_send.at[0, k, j], second_recv.at[0, k, j], along_x[j]))
            merge_part = merge.at[merge_rows(there)]
            relays.append(
                remote(merge_part, merge_part, second_send.at[1, k, j], second_recv.at[1, k, j], along_z[j])
            )
    for k in range(4):
        there = lanes_of(lax.rem(col + 2 * k, n_col))
        for j, part in enumerate((weight.at[:, :, there], merge.at[there])):
            twins.append(remote(part, part, twin_send.at[j, k], twin_recv.at[j, k], twin))
    for copy in quarters + wholes + keep:
        copy.start()

    @pl.loop(0, 6)
    def _(chunk):
        weight_copy(chunk).wait()
        source = region[inner, inner].reshape(784, 1280)
        packed = jnp.dot(source, packed_weight[chunk], preferred_element_type=jnp.float32)
        qkv[chunk, inner, inner] = packed.astype(jnp.bfloat16).reshape(7, 7, SUB, GROUP)

    for copy in quarters:
        copy.wait_recv()
    for copy in relays:
        copy.start()
    for copy in halo:
        copy.wait_recv()

    @pl.loop(0, 6)
    def _(chunk):
        source = jnp.concatenate(
            [region[0, pl.ds(0, 8)].reshape(128, 1280), region[inner, 0].reshape(112, 1280)], axis=0
        )
        packed = jnp.dot(source, packed_weight[chunk], preferred_element_type=jnp.float32).astype(jnp.bfloat16)
        qkv[chunk, 0] = packed[0:128].reshape(8, SUB, GROUP)
        qkv[chunk, inner, 0] = packed[128:240].reshape(7, SUB, GROUP)

    key_at = lax.broadcasted_iota(jnp.int32, (64, 128), 1) % 64
    query_at = lax.broadcasted_iota(jnp.int32, (64, 128), 0)
    row_cut = (key_at // 32 != query_at // 32) & (row == 0)
    col_cut = ((key_at // 16) % 2 != (query_at // 16) % 2) & (col == 0)

    def bias_of(cut):
        return jnp.where(cut, -1e30, 0.0)

    for group in range(2):
        window_pairs(qkv, group, (0, 0), mixed, bias_of(row_cut | col_cut))

    @pl.loop(1, 4)
    def _(a):
        for group in range(2):
            window_pairs(qkv, group, (0, 2 * a), mixed, bias_of(row_cut))
            window_pairs(qkv, group, (2 * a, 0), mixed, bias_of(col_cut))

    both = pl.ds(0, 2)
    back = [
        remote(mixed.at[both, 0, inner], mixed.at[both, 8, inner], back_send.at[0], back_recv.at[0], behind[0]),
        remote(mixed.at[both, inner, 0], mixed.at[both, inner, 8], back_send.at[1], back_recv.at[1], behind[1]),
        remote(mixed.at[both, 0, 0], mixed.at[both, 8, 8], back_send.at[2], back_recv.at[2], behind[2]),
    ]
    for copy in back:
        copy.start()

    @pl.loop(1, 4)
    def _(a):
        for b in range(1, 4):
            for group in range(2):
                window_pairs(qkv, group, (2 * a, 2 * b), mixed, None)

    out_weight_copy.wait()
    backward = strip_perm(True)
    for copy in back:
        copy.wait_recv()

    width = tokens.shape[2]
    slots = 8 * KSLOT
    ids = jnp.concatenate(
        [jnp.broadcast_to(parcel_ref[u : u + 1, :], (KSLOT, KSLOT)) for u in range(8)], axis=0
    )
    at = lax.broadcasted_iota(jnp.int32, (slots, KSLOT), 1) == lax.rem(
        lax.broadcasted_iota(jnp.int32, (slots, KSLOT), 0), KSLOT
    )
    ids = jnp.sum(jnp.where(at, ids.astype(jnp.float32), 0.0), axis=1, keepdims=True)
    live = ids >= 0
    ids = jnp.maximum(ids, 0.0)
    ids_high = jnp.floor(ids * (1.0 / 128.0))
    ids_low = ids - ids_high * 128.0
    place = place_ref[...]
    owner = picked(ids_high, ids_low, (place // 128).astype(jnp.float32))
    local = picked(ids_high, ids_low, (place % 128).astype(jnp.float32))
    kind = picked(owner, local, class_ref[...].astype(jnp.float32))
    power = exponent_of(kind, exponents)
    owner = jnp.where(live, owner, -1.0)
    owner_row = onto_rows(owner, slots)
    earlier = lax.broadcasted_iota(jnp.int32, (slots, slots), 1) < lax.broadcasted_iota(
        jnp.int32, (slots, slots), 0
    )
    rank = jnp.sum(jnp.where((owner == owner_row) & earlier, 1.0, 0.0), axis=1, keepdims=True)
    target = jnp.where(live, owner * 2.0 + rank, -1.0)
    target_row = onto_rows(target, slots)
    lane = lax.broadcasted_iota(jnp.int32, (KSLOT, META), 1)
    def pool_strip(strip, tile):
        cut = slice(KSLOT * strip, KSLOT * strip + KSLOT)
        match = (
            lax.broadcasted_iota(jnp.int32, (KSLOT, BLOCK), 0) == jnp.concatenate([slot_ref[4 * strip + i : 4 * strip + i + 1, :] for i in range(4)], axis=1)
        ).astype(jnp.float32)
        token_power = onto_columns(jnp.sum(match * power[cut], axis=0, keepdims=True), BLOCK)
        values = jnp.maximum(tile.astype(jnp.float32), pool_floor)
        lifted = jnp.exp(token_power * jnp.log(values))
        sums[cut, 0:width] = jnp.dot(
            match.astype(jnp.bfloat16), lifted.astype(jnp.bfloat16), preferred_element_type=jnp.float32
        )
        count = jnp.sum(match, axis=1, keepdims=True)
        sums[cut, width : width + META] = jnp.where(
            lane == 0, count, jnp.where(lane == 1, local[cut], 0.0)
        )

    for part in range(4):
        sources = []
        for half in range(2):
            strip = 2 * part + half
            packed = jnp.concatenate(
                [mixed[g, strip + 1, pl.ds(1, 8)].reshape(BLOCK, GROUP) for g in range(2)], axis=1
            )
            sources.append(jnp.dot(backward, packed, preferred_element_type=jnp.float32).astype(jnp.bfloat16))
        layer_out = jnp.dot(
            jnp.concatenate(sources, axis=0), out_weight[...], preferred_element_type=jnp.float32
        )
        for half in range(2):
            strip = 2 * part + half
            tile = (
                layer_out[BLOCK * half : BLOCK * half + BLOCK] + tokens[strip].astype(jnp.float32)
            ).astype(jnp.bfloat16)
            tokens[strip] = tile
            pool_strip(strip, tile)
    for strip in range(8):
        result_copy(strip).start()

    chooser = (
        lax.broadcasted_iota(jnp.int32, (256, slots), 0).astype(jnp.float32) == target_row
    ).astype(jnp.bfloat16)
    parts = range(len(CUTS))
    sends_a, recvs_a = (send_a0, send_a1, send_a2, send_a3,), (recv_a0, recv_a1, recv_a2, recv_a3,)
    sends_b, recvs_b = (send_b0, send_b1, send_b2, send_b3,), (recv_b0, recv_b1, recv_b2, recv_b3,)
    copies_a, copies_b = [], []
    for part in parts:
        rows = jnp.dot(chooser, sums[:, CUTS[part][0] : CUTS[part][1]].astype(jnp.bfloat16), preferred_element_type=jnp.float32)
        sends_a[part][...] = rows.astype(jnp.bfloat16).reshape(sends_a[part].shape)
        copies_a.append(exchange("tr", row, down, sends_a[part], recvs_a[part], send_sem_a.at[part], recv_sem_a.at[part]))
        recvs_a[part][row] = sends_a[part][row]

    def lists(at, count):
        return [adjacency[j, at * 8 + e] for e in range(8) for j in range(1, NB)]

    @pl.loop(0, 16)
    def _(there):
        least, most = jnp.int32(8), jnp.int32(-1)
        for block in lists(there, 8):
            inner_at = block - 8 * row
            mine = (inner_at >= 0) & (inner_at < 8)
            least = jnp.where(mine, jnp.minimum(least, inner_at), least)
            most = jnp.where(mine, jnp.maximum(most, inner_at), most)
        pick_out[there, 0] = jnp.minimum(least, 7)
        pick_out[there, 1] = jnp.maximum(most, 0)

    @pl.loop(0, 8)
    def _(e):
        named = lists(row, 8)
        for j in range(NB - 1):
            block = adjacency[j + 1, row * 8 + e]
            source = block // 8
            least = block
            for other in named:
                least = jnp.where(other // 8 == source, jnp.minimum(least, other), least)
            pick_in[e, j] = source * MAXB + jnp.where(block == least, 0, 1)

    for copy in quarters:
        copy.wait_send()
    for copy in wholes + relays:
        copy.wait()
    for copy in keep:
        copy.wait()
    for copy in twins:
        copy.start()
    out_at = lax.broadcasted_iota(jnp.int32, (256, 256), 0)
    in_at = lax.broadcasted_iota(jnp.int32, (256, 256), 1)
    swap = jnp.where(((out_at // 2) % 16) * 16 + (out_at // 32) * 2 + out_at % 2 == in_at, 1.0, 0.0)
    swap = swap.astype(jnp.bfloat16)
    for part in parts:
        for copy in copies_a[part]:
            copy.wait_recv()
        arrived = recvs_a[part][...]
        rows = jnp.dot(swap, arrived.reshape(256, arrived.shape[2]), preferred_element_type=jnp.float32)
        sends_b[part][...] = rows.astype(jnp.bfloat16).reshape(sends_b[part].shape)
        copies_b.append(exchange("tc", col, across, sends_b[part], recvs_b[part], send_sem_b.at[part], recv_sem_b.at[part]))
        recvs_b[part][col] = sends_b[part][col]
    own_kind = class_ref[pl.ds(row * n_col + col, 1), :].astype(jnp.float32)
    own_power = onto_columns(exponent_of(own_kind, exponents), PARCELS_DEV)
    lane = lax.broadcasted_iota(jnp.int32, (256, PARCELS_DEV), 1).astype(jnp.float32)
    embed_copy.wait()
    placed = None
    pooled = []
    for part in parts:
        for copy in copies_b[part]:
            copy.wait_recv()
        arrived = recvs_b[part][...]
        arrived = arrived.reshape(256, arrived.shape[2])
        if part == 0:
            split = arrived.shape[1] - META
            info = arrived[:, split:].astype(jnp.float32)
            count, local = info[:, 0:1], info[:, 1:2]
            placed = jnp.where((lane == local) & (count > 0), 1.0, 0.0).astype(jnp.bfloat16)
        total = lax.dot_general(placed, arrived, (((0,), (0,)), ((), ())), preferred_element_type=jnp.float32)
        if part == 0:
            counts = total[:, split : split + 1]
            total = total[:, 0:split]
        pooled.append(jnp.exp(jnp.log(total / counts) / own_power).astype(jnp.bfloat16))
    hidden = jnp.dot(
        jnp.concatenate(pooled[1:] + pooled[:1], axis=1), embed[...], preferred_element_type=jnp.float32
    ).astype(jnp.bfloat16)
    normed = layer_norm(hidden.astype(jnp.float32), parcel_gain[...].reshape(1, 1024)).astype(jnp.bfloat16)

    recv_1 = (recv_1_0, recv_1_1, recv_1_2, recv_1_3,)
    recv_2 = (recv_2_0, recv_2_1, recv_2_2, recv_2_3,)
    copies_1, copies_2, copies_3 = [], [], []
    for piece in range(PIECES):
        cut = slice(PIECE * piece, PIECE * piece + PIECE)
        for part in range(8):
            send_1[piece, part] = normed[cut, P_HDIM * part : P_HDIM * part + P_HDIM]
        copies_1.append(
            exchange("tc", col, across, send_1.at[piece], recv_1[piece], send_sem_1.at[piece], recv_sem_1.at[piece])
        )
        recv_1[piece][col] = send_1[piece, col]
    for piece in range(PIECES):
        for copy in copies_1[piece]:
            copy.wait_recv()
        for peer in down:
            there = peer["tr"]
            for slot in range(MAXB):
                send_2[piece, there, slot] = recv_1[piece][pick_out[there, slot]]
        copies_2.append(
            exchange("tr", row, down, send_2.at[piece], recv_2[piece], send_sem_2.at[piece], recv_sem_2.at[piece])
        )
        recv_2[piece][row] = jnp.zeros((MAXB, PIECE, P_HDIM), jnp.bfloat16)
    for copy in twins:
        copy.wait()
    query = jnp.dot(normed, weight[0], preferred_element_type=jnp.float32).astype(jnp.bfloat16)
    keys[0:PB] = jnp.dot(normed, weight[1], preferred_element_type=jnp.float32).astype(jnp.bfloat16)
    vals[0:PB] = jnp.dot(normed, weight[2], preferred_element_type=jnp.float32).astype(jnp.bfloat16)
    for piece in range(PIECES):
        for copy in copies_2[piece]:
            copy.wait_recv()
        for there in range(8):
            for j in range(NB - 1):
                at = pick_in[there, j]
                send_3[piece, there, j] = recv_2[piece][at // MAXB, at % MAXB]
        copies_3.append(
            exchange("tc", col, across, send_3.at[piece], recv_3.at[piece], send_sem_3.at[piece], recv_sem_3.at[piece])
        )
        recv_3[piece, col] = send_3[piece, col]
    near = (NB - 1) * PIECE
    for piece in range(PIECES):
        for copy in copies_3[piece]:
            copy.wait_recv()
        source = jnp.concatenate([recv_3[piece, part].reshape(near, P_HDIM) for part in range(8)], axis=1)
        cut = slice(PB + near * piece, PB + near * piece + near)
        keys[cut] = jnp.dot(source, weight[1], preferred_element_type=jnp.float32).astype(jnp.bfloat16)
        vals[cut] = jnp.dot(source, weight[2], preferred_element_type=jnp.float32).astype(jnp.bfloat16)
    attended = []
    for head in range(8):
        cut = slice(P_HDIM * head, P_HDIM * head + P_HDIM)
        scores = lax.dot_general(
            query[:, cut], keys[:, cut], (((1,), (1,)), ((), ())), preferred_element_type=jnp.float32
        ) * P_HDIM ** (-0.5)
        weights = softmax_rows(scores).astype(jnp.bfloat16)
        attended.append(
            jnp.dot(weights, vals[:, cut], preferred_element_type=jnp.float32).astype(jnp.bfloat16)
        )
    combined = jnp.dot(
        jnp.concatenate(attended, axis=1), merge[...], preferred_element_type=jnp.float32
    )
    out_ref[...] = (combined + hidden.astype(jnp.float32)).astype(jnp.bfloat16)
    for strip in range(8):
        result_copy(strip).wait()
    for copies in [halo, back] + copies_a + copies_b + copies_1 + copies_2 + copies_3:
        for copy in copies:
            copy.wait_send()


def hand_over_kernel(tile_from, vector_from, tile_to, vector_to, tile_here, vector_here, sem):
    pairs = [(tile_from.at[i], tile_here.at[i], tile_to.at[i]) for i in range(8)]
    pairs.append((vector_from, vector_here, vector_to))
    taken = [pltpu.make_async_copy(pair[0], pair[1], sem.at[0, i]) for i, pair in enumerate(pairs)]
    given = [pltpu.make_async_copy(pair[1], pair[2], sem.at[1, i]) for i, pair in enumerate(pairs)]
    for copy in taken:
        copy.start()
    for first, second in zip(taken, given):
        first.wait()
        second.start()
    for copy in given:
        copy.wait()


def hand_over(tile, vector):
    far = pl.BlockSpec(memory_space=pltpu.HBM)
    return pl.pallas_call(
        hand_over_kernel,
        out_shape=(jax.ShapeDtypeStruct(tile.shape, tile.dtype), jax.ShapeDtypeStruct(vector.shape, vector.dtype)),
        in_specs=[far, far],
        out_specs=(far, far),
        scratch_shapes=[
            pltpu.VMEM(tile.shape, tile.dtype),
            pltpu.VMEM(vector.shape, vector.dtype),
            pltpu.SemaphoreType.DMA((2, 9)),
        ],
        compiler_params=pltpu.CompilerParams(vmem_limit_bytes=62 * 1024 * 1024),
        name="hand_over",
    )(tile, vector)


def body(
    tokens,
    norm_gain,
    window_weight,
    output_weight,
    token_slot,
    block_parcel,
    parcel_place,
    parcel_class,
    pool_exponent,
    embed_weight,
    parcel_gain,
    parcel_weight,
    merge_weight,
    adjacency,
):
    width = tokens.shape[2]
    rows_out = embed_weight.shape[1]
    far = pl.BlockSpec(memory_space=pltpu.HBM)
    near = pl.BlockSpec(memory_space=pltpu.VMEM)
    scalars = pl.BlockSpec(memory_space=pltpu.SMEM)
    bf16 = jnp.bfloat16
    dma = pltpu.SemaphoreType.DMA
    tile, vector = pl.pallas_call(
        whole_kernel,
        out_shape=(
            jax.ShapeDtypeStruct((8, BLOCK, width), bf16),
            jax.ShapeDtypeStruct((PARCELS_DEV, rows_out), bf16),
        ),
        in_specs=[far, near, far, far, far, far, near, near, near, near, scalars, far, near, scalars],
        out_specs=(far, near),
        scratch_shapes=[
            pltpu.VMEM((8, BLOCK, width), bf16),
            pltpu.VMEM((9, 9, SUB, width), bf16),
            pltpu.VMEM((6, 8, 8, SUB, GROUP), bf16),
            pltpu.VMEM((2, 9, 9, SUB, GROUP), bf16),
            pltpu.VMEM((6, width, GROUP), bf16),
            pltpu.VMEM((width, width), bf16),
            pltpu.VMEM((3, rows_out, rows_out), bf16),
            pltpu.VMEM((rows_out, rows_out), bf16),
            pltpu.VMEM((width, rows_out), bf16),
            pltpu.VMEM((8 * KSLOT, width + META), jnp.float32),
            *[pltpu.VMEM((16, 16, high - low), bf16) for _ in range(2) for low, high in CUTS],
            *[pltpu.VMEM((8, 32, high - low), bf16) for _ in range(2) for low, high in CUTS],
            pltpu.VMEM((PIECES, 8, PIECE, P_HDIM), bf16),
            pltpu.VMEM((PIECES, 16, MAXB, PIECE, P_HDIM), bf16),
            pltpu.VMEM((PIECES, 8, NB - 1, PIECE, P_HDIM), bf16),
            pltpu.VMEM((PIECES, 8, NB - 1, PIECE, P_HDIM), bf16),
            pltpu.VMEM((NB * PB, rows_out), bf16),
            pltpu.VMEM((NB * PB, rows_out), bf16),
            pltpu.SMEM((16, MAXB), jnp.int32),
            pltpu.SMEM((8, NB - 1), jnp.int32),
            *[pltpu.VMEM((8, PIECE, P_HDIM), bf16) for _ in range(PIECES)],
            *[pltpu.VMEM((16, MAXB, PIECE, P_HDIM), bf16) for _ in range(PIECES)],
            dma((8,)),
            dma((8,)),
            dma((8,)),
            dma((3,)),
            dma((3,)),
            dma((3,)),
            dma((3,)),
            dma((2,)),
            dma((3, 3)),
            dma((3, 3)),
            dma((2, 3, 3)),
            dma((2, 3, 3)),
            dma((2, 4)),
            dma((2, 4)),
            dma((len(CUTS), 15)),
            dma((len(CUTS), 15)),
            dma((len(CUTS), 7)),
            dma((len(CUTS), 7)),
            dma((PIECES, 7)),
            dma((PIECES, 7)),
            dma((PIECES, 15)),
            dma((PIECES, 15)),
            dma((PIECES, 7)),
            dma((PIECES, 7)),
        ],
        compiler_params=pltpu.CompilerParams(
            collective_id=1, has_side_effects=True, vmem_limit_bytes=62 * 1024 * 1024
        ),
        cost_estimate=pl.CostEstimate(flops=20 * 10**9, bytes_accessed=30 * 10**6, transcendentals=5 * 10**6),
        name="encoder_and_parcels",
    )(
        tokens.reshape(8, BLOCK, width),
        norm_gain,
        window_weight,
        output_weight,
        parcel_weight,
        merge_weight,
        token_slot,
        block_parcel.reshape(8, KSLOT),
        parcel_place.reshape(128, 128),
        parcel_class.reshape(128, 128),
        pool_exponent,
        embed_weight,
        parcel_gain,
        adjacency.T,
    )
    tile, vector = hand_over(tile, vector)
    return (tile.reshape(tokens.shape), vector)


def solution(mesh):
    return jax.shard_map(
        body,
        mesh=mesh,
        in_specs=(
            P("tr", "tc", None),
            P(),
            P(),
            P(),
            P("tr", "tc"),
            P("tr", "tc", None),
            P(),
            P(),
            P(),
            P(),
            P(),
            P(None, None, "tc"),
            P("tc", None),
            P(),
        ),
        out_specs=(P("tr", "tc", None), P(("tr", "tc"), None)),
        check_vma=False,
    )
```
